256 devices in a mesh: grp: 32 (over z_lo, x, core), tp: 8 (over y, z_hi).
Axes of the slice: x: 4, y: 4, z: 8 (z_hi: 2, z_lo: 4; z = z_hi * 4 + z_lo), core: 2. Of those that a mesh axis runs over, the one named last changes fastest.
Arguments:
- states: bfloat16 [2, 2048, 8192], P(None, 'grp', 'tp'), may hold values from -6 to 6
- cache: bfloat16 [2, 2048, 8, 128, 128], P(None, 'grp', 'tp'), may hold values from -256 to 256
- lengths: int32 [2048], P('grp'), may hold values from 32 to 128, as said below
- plan: int32 [32], replicated, may hold values from 0 to 31, each once
- wq_new: bfloat16 [8192, 4096], P('grp', 'tp'), may hold values from -0.0625 to 0.0625
- wkv_new: bfloat16 [2, 8192, 1024], P(None, 'grp', 'tp'), may hold values from -0.0625 to 0.0625
- wo_new: bfloat16 [4096, 8192], P('tp', 'grp'), may hold values from -0.09375 to 0.09375
Outputs:
- attended: bfloat16 [2, 2048, 8192], P(None, 'grp', 'tp')
- new_kv: bfloat16 [2, 2, 2048, 8, 128], P(None, None, 'grp', 'tp')
The draws below stay inside these ranges and needn't reach their ends.
Inputs may be any that keep to these rules, and one draw needn't show every extreme that they name: `plan`: a permutation of the owners. `lengths`: some row of every draw has exactly 128.
All inputs are finite; a program needn't handle non-finite values.
Results may differ from the reference program's by a relative error of at most 0.017.
Values may be sent and summed in bfloat16 or wider, within the bound.
A program may use at most 128 MiB of HBM per device.

```python
import jax
import jax.numpy as jnp
from jax import lax

D = 8192
H = 32
KVH = 8
HD = 128
ROWS_G = 64
LEN = 128
ROWS = 2048
BLOCK = 256
N_GRP = 32


def draw_cache(key, part):
    key = jax.random.fold_in(key, 11)
    first, second = jax.random.split(key, 2)
    shape = (ROWS, KVH, LEN, HD)
    keys = 1.5 * jnp.clip(jax.random.normal(first, shape, jnp.float32), -5.0, 5.0)
    values = jnp.clip(jax.random.normal(second, shape, jnp.float32), -5.0, 5.0)
    return jnp.stack([keys, values]).astype(jnp.bfloat16)


def draw_lengths(key, part):
    key = jax.random.fold_in(key, 5)
    first, second = jax.random.split(key)
    base = jax.random.randint(first, (ROWS,), LEN // 4, LEN + 1)
    picked = jax.random.randint(second, (), 0, ROWS)
    return jnp.where(jnp.arange(ROWS) == picked, LEN, base).astype(jnp.int32)


def levels(own_key, shape, cuts, least, largest):
    gain = 1.0
    for dim, blocks in cuts:
        draws = jax.random.uniform(jax.random.fold_in(jax.random.fold_in(own_key, 6), dim), (blocks,), jnp.float32, least / len(cuts), largest / len(cuts))
        gain = gain * jnp.repeat(jnp.exp(draws), shape[dim] // blocks).reshape((-1,) + (1,) * (len(shape) - 1 - dim))
    return gain


def centred(own_key, extent, deviation, limit, pieces=(), kind=jnp.bfloat16):
    array = jax.random.normal(own_key, extent, jnp.float32) * deviation
    if len(pieces) > 0:
        array = levels(own_key, extent, pieces, -0.22, 0.18) * array
    return jnp.clip(array, min=-limit, max=limit).astype(kind)


def setup_inputs(seed: int = 0) -> dict:
    seeds = jax.random.split(jax.random.key(seed), 8)
    states = centred(seeds[0], (2, ROWS, D), 1.0, 6.0, ((1, 32), (2, 8)))
    cache = draw_cache(jax.random.fold_in(seeds[7], 71), 0)
    lengths = draw_lengths(jax.random.fold_in(seeds[7], 71), 0)
    plan = jax.random.permutation(seeds[3], N_GRP).astype(jnp.int32)
    wq_new = centred(seeds[4], (D, H * HD), D ** -0.5, 0.0625, ((0, 32), (1, 8)))
    wkv_new = centred(seeds[5], (2, D, KVH * HD), D ** -0.5, 0.0625, ((1, 32), (2, 8)))
    wo_new = centred(seeds[6], (H * HD, D), (H * HD) ** -0.5, 0.09375, ((0, 8), (1, 32)))
    return {"states": states, "cache": cache, "lengths": lengths, "plan": plan, "wq_new": wq_new, "wkv_new": wkv_new, "wo_new": wo_new}


def reference(states, cache, lengths, plan, wq_new, wkv_new, wo_new):
    inverse = jnp.argsort(plan).astype(jnp.int32)

    def true_rows(stored):
        return stored.reshape(N_GRP, BLOCK, -1)[inverse].reshape(D, -1)
    w_query = true_rows(wq_new)
    w_key = true_rows(wkv_new[0])
    w_value = true_rows(wkv_new[1])
    w_output = wo_new.reshape(H * HD, N_GRP, BLOCK)[:, inverse].reshape(H * HD, D)
    group = H // KVH
    scale = 1.0 / HD ** 0.5
    hp = lax.Precision.HIGHEST

    def one_group(index):
        first = (index * ROWS_G).astype(jnp.int32)
        block_states = lax.dynamic_slice_in_dim(states, first, ROWS_G, 1)
        block_cache = lax.dynamic_slice_in_dim(cache, first, ROWS_G, 1)
        block_lengths = lax.dynamic_slice_in_dim(lengths, first, ROWS_G, 0)
        widened = block_states.astype(jnp.float32)
        normed = (widened * lax.rsqrt(lax.optimization_barrier(jnp.mean(widened * widened, axis=-1, keepdims=True)) + 1e-05)).astype(jnp.bfloat16)
        normed = normed.reshape(2 * ROWS_G, D)
        query = jnp.dot(normed, w_query, preferred_element_type=jnp.float32).astype(jnp.bfloat16)
        query = query.reshape(2, ROWS_G, KVH, group, HD).astype(jnp.float32)
        key_new = jnp.dot(normed, w_key, preferred_element_type=jnp.float32).astype(jnp.bfloat16).reshape(2, ROWS_G, KVH, HD)
        value_new = jnp.dot(normed, w_value, preferred_element_type=jnp.float32).astype(jnp.bfloat16).reshape(2, ROWS_G, KVH, HD)
        keys = block_cache[0].astype(jnp.float32)
        values = block_cache[1].astype(jnp.float32)
        scores = jnp.einsum('srkgd,rkpd->srkgp', query, keys, precision=hp) * scale
        slots = lax.broadcasted_iota(jnp.int32, (ROWS_G, LEN), 1)
        valid = (slots < block_lengths.astype(jnp.int32)[:, None])[None, :, None, None, :]
        scores = jnp.where(valid, scores, -1e+30)
        own = jnp.einsum('srkgd,trkd->srkgt', query, key_new.astype(jnp.float32), precision=hp) * scale
        step_ids = lax.broadcasted_iota(jnp.int32, (2, 1, 1, 1, 2), 0)
        key_ids = lax.broadcasted_iota(jnp.int32, (2, 1, 1, 1, 2), 4)
        own = jnp.where(key_ids <= step_ids, own, -1e+30)
        top = jnp.maximum(lax.optimization_barrier(jnp.max(scores, axis=-1, keepdims=True)), lax.optimization_barrier(jnp.max(own, axis=-1, keepdims=True)))
        cached_exp = jnp.exp(scores - top)
        own_exp = jnp.exp(own - top)
        total = lax.optimization_barrier(jnp.sum(cached_exp, axis=-1, keepdims=True)) + lax.optimization_barrier(jnp.sum(own_exp, axis=-1, keepdims=True))
        cached_weight = (cached_exp / total).astype(jnp.bfloat16).astype(jnp.float32)
        own_weight = (own_exp / total).astype(jnp.bfloat16).astype(jnp.float32)
        heads = jnp.einsum('srkgp,rkpd->srkgd', cached_weight, values, precision=hp)
        heads = heads + jnp.einsum('srkgt,trkd->srkgd', own_weight, value_new.astype(jnp.float32), precision=hp)
        heads = heads.astype(jnp.bfloat16).reshape(2 * ROWS_G, H * HD)
        mixed = jnp.dot(heads, w_output, preferred_element_type=jnp.float32).astype(jnp.bfloat16)
        return (mixed.reshape(2, ROWS_G, D), jnp.stack([key_new, value_new], axis=1))
    mixed, fresh = lax.map(one_group, jnp.arange(N_GRP, dtype=jnp.int32))
    attended = jnp.transpose(mixed, (1, 0, 2, 3)).reshape(2, ROWS, D)
    new_kv = jnp.transpose(fresh, (1, 2, 0, 3, 4, 5)).reshape(2, 2, ROWS, KVH, HD)
    return (attended, new_kv)
```

```python
import functools

import jax
import jax.numpy as jnp
from jax import lax
from jax.experimental import pallas as pl
from jax.experimental.pallas import tpu as pltpu
from jax.sharding import PartitionSpec as P

MESH = pl.DeviceIdType.MESH
F32 = jnp.float32
BF16 = jnp.bfloat16


def kernel(
    plan, lengths, states, cache, wq, wkv, wo,
    out, new_kv,
    own_q, own_kv,
    wa, wb, st, xn, acc, keys, values, lens, q8, h8, heads, kvn, inverse,
    part, from_left, from_right, transit, far_out, far_in,
    local_sem, st_send, st_recv, w_send, w_recv, r_send, r_recv,
):
    grp = lax.axis_index("grp")
    tp = lax.axis_index("tp")
    z, x, c = grp // 8, lax.rem(grp // 2, 4), lax.rem(grp, 2)
    y, zh = tp // 2, lax.rem(tp, 2)

    def mod4(v):
        return lax.rem(v + 4, 4)

    def block_of(z_, x_, c_):
        return (z_ * 4 + x_) * 2 + c_

    def device(x_=x, y_=y, z_=z, zh_=zh, c_=c):
        return (block_of(z_, x_, c_), y_ * 2 + zh_)

    xl, xr, xo = mod4(x - 1), mod4(x + 1), mod4(x + 2)
    yl, yr, yo = mod4(y - 1), mod4(y + 1), mod4(y + 2)
    zk = [z, z + 1 - 2 * lax.rem(z, 2), mod4(z + 2), 3 - z]

    locals_ = [
        pltpu.make_async_copy(wq, own_q, local_sem.at[0]),
        pltpu.make_async_copy(wkv.at[0], own_kv.at[0], local_sem.at[1]),
        pltpu.make_async_copy(wkv.at[1], own_kv.at[1], local_sem.at[2]),
        pltpu.make_async_copy(states, st.at[tp], local_sem.at[3]),
        pltpu.make_async_copy(wo, wb.at[grp], local_sem.at[4]),
        pltpu.make_async_copy(cache.at[0], keys, local_sem.at[5]),
        pltpu.make_async_copy(cache.at[1], values, local_sem.at[6]),
    ]
    for copy in locals_:
        copy.start()

    partners = [
        device(x_=xl), device(x_=xr), device(c_=1 - c),
        device(y_=yl), device(y_=yr), device(y_=yo), device(zh_=1 - zh),
        device(z_=zk[1]), device(z_=zk[2]), device(z_=zk[3]),
    ]
    barrier = pltpu.get_barrier_semaphore()
    for partner in partners:
        pl.semaphore_signal(barrier, inc=1, device_id=partner, device_id_type=MESH)
    for i in (0, 1, 2):
        locals_[i].wait()
    wa[grp, :, 0:512] = own_q[...]
    wa[grp, :, 512:640] = own_kv[0]
    wa[grp, :, 640:768] = own_kv[1]
    pl.semaphore_wait(barrier, len(partners))

    sent = []

    def send(src, dst, send_sem, recv_sem, to):
        copy = pltpu.make_async_remote_copy(
            src_ref=src, dst_ref=dst, send_sem=send_sem, recv_sem=recv_sem,
            device_id=to, device_id_type=MESH,
        )
        copy.start()
        sent.append(copy)

    def arrived(dst, recv_sem):
        pltpu.make_async_remote_copy(
            src_ref=dst, dst_ref=dst, send_sem=recv_sem, recv_sem=recv_sem,
            device_id=device(c_=1 - c), device_id_type=MESH,
        ).wait_recv()

    stores = (wa, wb)
    halves = (128, 256)

    def z_sends(t):
        for k in (1, 2, 3):
            ref = stores[t].at[grp]
            send(ref, ref, w_send.at[t, k - 1], w_recv.at[t, k - 1], device(z_=zk[k]))

    def base(k):
        return 3 + 8 * k

    def sibling(t, k, i, ref):
        s = base(k) + 4 + i
        send(ref, ref, w_send.at[t, s], w_recv.at[t, s], device(c_=1 - c))

    def e1(t, k):
        ref = stores[t].at[block_of(zk[k], x, c)]
        if k:
            arrived(ref, w_recv.at[t, k - 1])
        s = base(k)
        send(ref, ref, w_send.at[t, s], w_recv.at[t, s], device(x_=xr))
        send(ref, ref, w_send.at[t, s + 1], w_recv.at[t, s + 1], device(x_=xl))
        sibling(t, k, 0, ref)

    def e2(t, k):
        s = base(k)
        half = halves[t]
        bl = block_of(zk[k], xl, c)
        ref = stores[t].at[bl]
        arrived(ref, w_recv.at[t, s])
        low = stores[t].at[bl, pl.ds(0, half)]
        send(low, low, w_send.at[t, s + 2], w_recv.at[t, s + 2], device(x_=xr))
        sibling(t, k, 1, ref)
        br = block_of(zk[k], xr, c)
        ref = stores[t].at[br]
        arrived(ref, w_recv.at[t, s + 1])
        high = stores[t].at[br, pl.ds(half, half)]
        send(high, high, w_send.at[t, s + 3], w_recv.at[t, s + 3], device(x_=xl))
        sibling(t, k, 2, ref)

    def e3(t, k):
        s = base(k)
        half = halves[t]
        bo = block_of(zk[k], xo, c)
        arrived(stores[t].at[bo, pl.ds(0, half)], w_recv.at[t, s + 2])
        arrived(stores[t].at[bo, pl.ds(half, half)], w_recv.at[t, s + 3])
        sibling(t, k, 3, stores[t].at[bo])

    def e4(t, k):
        for i, x_ in enumerate((x, xl, xr, xo)):
            s = base(k) + 4 + i
            arrived(stores[t].at[block_of(zk[k], x_, 1 - c)], w_recv.at[t, s])

    tp_far = y * 2 + 1 - zh

    def spread_states(first, t):
        for i, y_ in enumerate((yr, yl, yo)):
            send(st.at[t], st.at[t], st_send.at[first + i], st_recv.at[first + i], device(y_=y_))

    e1(0, 0)
    z_sends(0)
    locals_[3].wait()
    send(st.at[tp], st.at[tp], st_send.at[0], st_recv.at[0], device(zh_=1 - zh))
    spread_states(1, tp)
    locals_[4].wait()
    z_sends(1)

    acc[...] = jnp.zeros_like(acc)

    def one_length(r, carry):
        lens[pl.ds(r, 1), :] = jnp.full((1, 128), lengths[r], jnp.int32)
        return carry

    lax.fori_loop(0, 64, one_length, 0)

    def one_inverse(tb, carry):
        def look(b, found):
            return jnp.maximum(found, jnp.where(plan[b] == tb, b, 0))

        inverse[tb] = lax.fori_loop(0, 32, look, jnp.int32(0), unroll=8)
        return carry

    lax.fori_loop(0, 32, one_inverse, 0)

    e2(0, 0)
    e1(0, 1)
    arrived(st.at[tp_far], st_recv.at[0])
    spread_states(4, tp_far)
    e1(0, 2)
    e3(0, 0)
    e2(0, 1)
    e1(0, 3)
    e3(0, 1)

    for first, zh_ in ((1, zh), (4, 1 - zh)):
        for i, y_ in enumerate((yl, yr, yo)):
            arrived(st.at[y_ * 2 + zh_], st_recv.at[first + i])

    def squares(t, total):
        wide = st[t].astype(F32)
        return total + jnp.sum(wide * wide, axis=-1, keepdims=True)

    total = lax.fori_loop(0, 8, squares, jnp.zeros((128, 1), F32))
    gain = lax.rsqrt(total / 8192.0 + 1e-05)

    def normalise(t, carry):
        for j in range(4):
            wide = st[t, :, 256 * j : 256 * (j + 1)].astype(F32)
            xn[t * 4 + j] = (wide * gain).astype(BF16)
        return carry

    lax.fori_loop(0, 8, normalise, 0)

    def project(k):

        def one(i, carry):
            b = zk[k] * 8 + i
            left = xn[plan[b]]
            acc[...] += jnp.dot(left, wa[b], preferred_element_type=F32)
            return carry

        lax.fori_loop(0, 8, one, 0)

    e2(0, 2)
    e1(1, 0)
    e3(0, 2)
    e2(0, 3)
    e1(1, 1)
    e3(0, 3)
    e1(1, 2)
    for k in range(4):
        e4(0, k)
    for k in range(4):
        project(k)

    for s in range(2):
        rows = slice(64 * s, 64 * (s + 1))
        for g in range(4):
            piece = acc[rows, 128 * g : 128 * (g + 1)]
            q8[:, 4 * s + g, :] = piece.astype(BF16).astype(F32)
        for i in range(2):
            piece = acc[rows, 512 + 128 * i : 640 + 128 * i].astype(BF16)
            new_kv[s, i] = piece
            kvn[s, i] = piece.astype(F32)
    locals_[5].wait()
    locals_[6].wait()
    scale = 1.0 / 128**0.5

    def attend(n):
        rows = pl.ds(16 * n, 16)
        q = q8[rows]
        score = lax.dot_general(
            q.astype(BF16), keys[rows], (((2,), (2,)), ((0,), (0,))), preferred_element_type=F32
        ) * scale
        slots = lax.broadcasted_iota(jnp.int32, (16, 8, 128), 2)
        score = jnp.where(slots < lens[rows][:, None, :], score, -1e30)
        own = [
            jnp.sum(q * kvn[t, 0, rows][:, None, :], axis=-1, keepdims=True) * scale
            for t in range(2)
        ]
        second = lax.broadcasted_iota(jnp.int32, (16, 8, 1), 1) >= 4
        own[1] = jnp.where(second, own[1], -1e30)
        top = jnp.maximum(jnp.max(score, axis=-1, keepdims=True), jnp.maximum(own[0], own[1]))
        cached = jnp.exp(score - top)
        fresh = [jnp.exp(o - top) for o in own]
        total = jnp.sum(cached, axis=-1, keepdims=True) + fresh[0] + fresh[1]
        weight = (cached / total).astype(BF16)
        result = lax.dot_general(
            weight, values[rows], (((2,), (1,)), ((0,), (0,))), preferred_element_type=F32
        )
        for t in range(2):
            w = (fresh[t] / total).astype(BF16).astype(F32)
            result = result + w * kvn[t, 1, rows][:, None, :]
        h8[rows] = result

    attend(0)
    attend(1)
    e2(1, 0)
    e1(1, 3)
    attend(2)
    attend(3)
    e3(1, 0)
    for s in range(2):
        for g in range(4):
            heads[64 * s : 64 * (s + 1), 128 * g : 128 * (g + 1)] = h8[:, 4 * s + g, :].astype(BF16)
    e2(1, 1)
    e3(1, 1)
    e2(1, 2)
    e3(1, 2)
    e2(1, 3)
    e3(1, 3)
    for k in range(4):
        e4(1, k)

    def product(j, t):
        right = wb[inverse[t * 4 + j]]
        part[j, t] = jnp.dot(heads[...], right, preferred_element_type=F32).astype(BF16)

    def r_send_to(j, i, src, dst, to):
        send(src, dst, r_send.at[j, i], r_recv.at[j, i], to)

    to_left, to_right = device(y_=yl), device(y_=yr)
    for j in range(4):
        product(j, yo * 2)
        r_send_to(j, 0, part.at[j, yo * 2], transit.at[j, 0], to_right)
        product(j, yo * 2 + 1)
        r_send_to(j, 1, part.at[j, yo * 2 + 1], transit.at[j, 1], to_left)
        product(j, yr * 2 + 1)
        r_send_to(j, 2, part.at[j, yr * 2 + 1], from_left.at[j, 1], to_right)
        product(j, yl * 2)
        r_send_to(j, 3, part.at[j, yl * 2], from_right.at[j, 0], to_left)
        product(j, yr * 2)
        product(j, yl * 2 + 1)
        product(j, y * 2)
        product(j, y * 2 + 1)

    def add(j, t, i):
        part[j, t] = (part[j, t].astype(F32) + transit[j, i].astype(F32)).astype(BF16)

    for j in range(4):
        arrived(transit.at[j, 0], r_recv.at[j, 0])
        add(j, yr * 2, 0)
        r_send_to(j, 4, part.at[j, yr * 2], from_left.at[j, 0], to_right)
        arrived(transit.at[j, 1], r_recv.at[j, 1])
        add(j, yl * 2 + 1, 1)
        r_send_to(j, 5, part.at[j, yl * 2 + 1], from_right.at[j, 1], to_left)

    def summed(j, h):
        return (
            part[j, y * 2 + h].astype(F32) + from_left[j, h].astype(F32) + from_right[j, h].astype(F32)
        )

    for j in range(4):
        arrived(from_left.at[j, 1], r_recv.at[j, 2])
        arrived(from_right.at[j, 0], r_recv.at[j, 3])
        arrived(from_left.at[j, 0], r_recv.at[j, 4])
        arrived(from_right.at[j, 1], r_recv.at[j, 5])
        far_out[j] = summed(j, 1 - zh).astype(BF16)
        r_send_to(j, 6, far_out.at[j], far_in.at[j], device(zh_=1 - zh))
    for j in range(4):
        arrived(far_in.at[j], r_recv.at[j, 6])
        out[:, 256 * j : 256 * (j + 1)] = (summed(j, zh) + far_in[j].astype(F32)).astype(BF16)

    for copy in sent:
        copy.wait_send()


def on_device(states, cache, lengths, plan, wq_new, wkv_new, wo_new):
    vmem = pltpu.VMEM
    dma = pltpu.SemaphoreType.DMA
    hbm = pl.BlockSpec(memory_space=pltpu.HBM)
    smem = pl.BlockSpec(memory_space=pltpu.SMEM)
    attended, new_kv = pl.pallas_call(
        kernel,
        out_shape=(
            jax.ShapeDtypeStruct((128, 1024), BF16),
            jax.ShapeDtypeStruct((2, 2, 64, 128), BF16),
        ),
        in_specs=[smem, smem, hbm, hbm, hbm, hbm, hbm],
        out_specs=[pl.BlockSpec(memory_space=pltpu.VMEM)] * 2,
        scratch_shapes=[
            vmem((256, 512), BF16),
            vmem((2, 256, 128), BF16),
            vmem((32, 256, 768), BF16),
            vmem((32, 512, 256), BF16),
            vmem((8, 128, 1024), BF16),
            vmem((32, 128, 256), BF16),
            vmem((128, 768), F32),
            vmem((64, 128, 128), BF16),
            vmem((64, 128, 128), BF16),
            vmem((64, 128), jnp.int32),
            vmem((64, 8, 128), F32),
            vmem((64, 8, 128), F32),
            vmem((128, 512), BF16),
            vmem((2, 2, 64, 128), F32),
            pltpu.SMEM((32,), jnp.int32),
            vmem((4, 8, 128, 256), BF16),
            vmem((4, 2, 128, 256), BF16),
            vmem((4, 2, 128, 256), BF16),
            vmem((4, 2, 128, 256), BF16),
            vmem((4, 128, 256), BF16),
            vmem((4, 128, 256), BF16),
            dma((7,)),
            dma((7,)), dma((7,)),
            dma((2, 35)), dma((2, 35)),
            dma((4, 7)), dma((4, 7)),
        ],
        compiler_params=pltpu.CompilerParams(
            collective_id=0, has_side_effects=True, vmem_limit_bytes=60 * 2**20
        ),
        name="layer",
    )(
        plan, lengths, states.reshape(128, 1024), cache.reshape(2, 64, 128, 128),
        wq_new, wkv_new, wo_new,
    )
    return attended.reshape(2, 64, 1024), new_kv.reshape(2, 2, 64, 1, 128)


def solution(mesh):
    return jax.shard_map(
        on_device,
        mesh=mesh,
        in_specs=(
            P(None, "grp", "tp"),
            P(None, "grp", "tp", None, None),
            P("grp"),
            P(),
            P("grp", "tp"),
            P(None, "grp", "tp"),
            P("tp", "grp"),
        ),
        out_specs=(P(None, "grp", "tp"), P(None, None, "grp", "tp", None)),
        check_vma=False,
    )
```

```python
import functools

import jax
import jax.numpy as jnp
from jax import lax
from jax.experimental import pallas as pl
from jax.experimental.pallas import tpu as pltpu
from jax.sharding import PartitionSpec as P

MESH = pl.DeviceIdType.MESH
F32 = jnp.float32
BF16 = jnp.bfloat16


def kernel(
    plan, lengths, states, cache, wq, wkv, wo,
    out, new_kv,
    own_q, own_kv,
    wa, wb, st, xn, acc, keys, values, lens, q8, h8, heads, kvn, inverse,
    part, from_left, from_right, transit, far_out, far_in,
    local_sem, st_send, st_recv, w_send, w_recv, z_send, r_send, r_recv,
):
    grp = lax.axis_index("grp")
    tp = lax.axis_index("tp")
    z, x, c = grp // 8, lax.rem(grp // 2, 4), lax.rem(grp, 2)
    y, zh = tp // 2, lax.rem(tp, 2)

    def mod4(v):
        return lax.rem(v + 4, 4)

    def block_of(z_, x_, c_):
        return (z_ * 4 + x_) * 2 + c_

    def device(x_=x, y_=y, z_=z, zh_=zh, c_=c):
        return (block_of(z_, x_, c_), y_ * 2 + zh_)

    xl, xr, xo = mod4(x - 1), mod4(x + 1), mod4(x + 2)
    yl, yr, yo = mod4(y - 1), mod4(y + 1), mod4(y + 2)
    z_pair, z_mirror = z + 1 - 2 * lax.rem(z, 2), 3 - z
    upper = z // 2
    inner = lax.rem(z + 1, 4) // 2 == 1
    zk = [z, z_pair, 2 - upper, 3 - 3 * upper]

    locals_ = [
        pltpu.make_async_copy(wq, own_q, local_sem.at[0]),
        pltpu.make_async_copy(wkv.at[0], own_kv.at[0], local_sem.at[1]),
        pltpu.make_async_copy(wkv.at[1], own_kv.at[1], local_sem.at[2]),
        pltpu.make_async_copy(states, st.at[tp], local_sem.at[3]),
        pltpu.make_async_copy(wo, wb.at[grp], local_sem.at[4]),
        pltpu.make_async_copy(cache.at[0], keys, local_sem.at[5]),
        pltpu.make_async_copy(cache.at[1], values, local_sem.at[6]),
    ]
    for copy in locals_:
        copy.start()

    partners = [
        device(x_=xl), device(x_=xr), device(c_=1 - c),
        device(y_=yl), device(y_=yr), device(y_=yo), device(zh_=1 - zh),
        device(z_=z_pair), device(z_=z_mirror),
    ]
    barrier = pltpu.get_barrier_semaphore()
    for partner in partners:
        pl.semaphore_signal(barrier, inc=1, device_id=partner, device_id_type=MESH)
    for i in (0, 1, 2):
        locals_[i].wait()
    wa[grp, :, 0:512] = own_q[...]
    wa[grp, :, 512:640] = own_kv[0]
    wa[grp, :, 640:768] = own_kv[1]
    pl.semaphore_wait(barrier, len(partners))

    sent = []

    def send(src, dst, send_sem, recv_sem, to):
        copy = pltpu.make_async_remote_copy(
            src_ref=src, dst_ref=dst, send_sem=send_sem, recv_sem=recv_sem,
            device_id=to, device_id_type=MESH,
        )
        copy.start()
        sent.append(copy)

    def arrived(dst, recv_sem):
        pltpu.make_async_remote_copy(
            src_ref=dst, dst_ref=dst, send_sem=recv_sem, recv_sem=recv_sem,
            device_id=device(c_=1 - c), device_id_type=MESH,
        ).wait_recv()

    stores = (wa, wb)
    halves = (128, 256)

    inner_sent = []

    def z_start(t):
        ref = stores[t].at[grp]
        send(ref, ref, w_send.at[t, 0], w_recv.at[t, 0], device(z_=z_pair))
        z_cross(t, 0)

    def z_cross(t, k):
        ref = stores[t].at[block_of(zk[k], x, c)]
        to = device(z_=z_mirror) if k < 2 else device(z_=z_pair)
        arrives = 1 + k if k < 2 else k - 1
        copy = pltpu.make_async_remote_copy(
            src_ref=ref, dst_ref=ref, send_sem=z_send.at[t, k], recv_sem=w_recv.at[t, arrives],
            device_id=to, device_id_type=MESH,
        )
        pl.when(inner)(copy.start)
        inner_sent.append(copy)

    def z_next(t, k):
        arrived(stores[t].at[block_of(zk[k], x, c)], w_recv.at[t, k - 1])
        z_cross(t, k)

    def base(k):
        return 3 + 8 * k

    def sibling(t, k, i, ref):
        s = base(k) + 4 + i
        send(ref, ref, w_send.at[t, s], w_recv.at[t, s], device(c_=1 - c))

    def e1(t, k):
        ref = stores[t].at[block_of(zk[k], x, c)]
        s = base(k)
        send(ref, ref, w_send.at[t, s], w_recv.at[t, s], device(x_=xr))
        send(ref, ref, w_send.at[t, s + 1], w_recv.at[t, s + 1], device(x_=xl))
        sibling(t, k, 0, ref)

    def e2(t, k):
        s = base(k)
        half = halves[t]
        bl = block_of(zk[k], xl, c)
        ref = stores[t].at[bl]
        arrived(ref, w_recv.at[t, s])
        low = stores[t].at[bl, pl.ds(0, half)]
        send(low, low, w_send.at[t, s + 2], w_recv.at[t, s + 2], device(x_=xr))
        sibling(t, k, 1, ref)
        br = block_of(zk[k], xr, c)
        ref = stores[t].at[br]
        arrived(ref, w_recv.at[t, s + 1])
        high = stores[t].at[br, pl.ds(half, half)]
        send(high, high, w_send.at[t, s + 3], w_recv.at[t, s + 3], device(x_=xl))
        sibling(t, k, 2, ref)

    def e3(t, k):
        s = base(k)
        half = halves[t]
        bo = block_of(zk[k], xo, c)
        arrived(stores[t].at[bo, pl.ds(0, half)], w_recv.at[t, s + 2])
        arrived(stores[t].at[bo, pl.ds(half, half)], w_recv.at[t, s + 3])
        sibling(t, k, 3, stores[t].at[bo])

    def e4(t, k):
        for i, x_ in enumerate((x, xl, xr, xo)):
            s = base(k) + 4 + i
            arrived(stores[t].at[block_of(zk[k], x_, 1 - c)], w_recv.at[t, s])

    tp_far = y * 2 + 1 - zh

    def spread_states(first, t):
        for i, y_ in enumerate((yr, yl, yo)):
            send(st.at[t], st.at[t], st_send.at[first + i], st_recv.at[first + i], device(y_=y_))

    e1(0, 0)
    z_start(0)
    locals_[3].wait()
    spread_states(1, tp)

    acc[...] = jnp.zeros_like(acc)

    def one_length(r, carry):
        lens[pl.ds(r, 1), :] = jnp.full((1, 128), lengths[r], jnp.int32)
        return carry

    lax.fori_loop(0, 64, one_length, 0)

    def one_inverse(tb, carry):
        def look(b, found):
            return jnp.maximum(found, jnp.where(plan[b] == tb, b, 0))

        inverse[tb] = lax.fori_loop(0, 32, look, jnp.int32(0), unroll=8)
        return carry

    lax.fori_loop(0, 32, one_inverse, 0)

    z_next(0, 1)
    e1(0, 1)
    e2(0, 0)
    z_next(0, 2)
    e1(0, 2)
    send(st.at[tp], st.at[tp], st_send.at[0], st_recv.at[0], device(zh_=1 - zh))
    e3(0, 0)
    z_next(0, 3)
    e2(0, 1)
    e1(0, 3)
    locals_[4].wait()
    z_start(1)
    arrived(st.at[tp_far], st_recv.at[0])
    spread_states(4, tp_far)
    e3(0, 1)
    z_next(1, 1)
    e2(0, 2)
    e1(1, 0)
    z_next(1, 2)
    e3(0, 2)
    z_next(1, 3)

    for first, zh_ in ((1, zh), (4, 1 - zh)):
        for i, y_ in enumerate((yl, yr, yo)):
            arrived(st.at[y_ * 2 + zh_], st_recv.at[first + i])

    def squares(t, total):
        wide = st[t].astype(F32)
        return total + jnp.sum(wide * wide, axis=-1, keepdims=True)

    total = lax.fori_loop(0, 8, squares, jnp.zeros((128, 1), F32))
    gain = lax.rsqrt(total / 8192.0 + 1e-05)

    def normalise(t, carry):
        for j in range(4):
            wide = st[t, :, 256 * j : 256 * (j + 1)].astype(F32)
            xn[t * 4 + j] = (wide * gain).astype(BF16)
        return carry

    lax.fori_loop(0, 8, normalise, 0)

    def project(k):

        def one(i, carry):
            b = zk[k] * 8 + i
            left = xn[plan[b]]
            acc[...] += jnp.dot(left, wa[b], preferred_element_type=F32)
            return carry

        lax.fori_loop(0, 8, one, 0)

    e2(0, 3)
    e1(1, 1)
    e3(0, 3)
    e1(1, 2)
    e2(1, 0)
    e1(1, 3)
    for k in range(4):
        e4(0, k)
    for k in range(4):
        project(k)

    for s in range(2):
        rows = slice(64 * s, 64 * (s + 1))
        for g in range(4):
            piece = acc[rows, 128 * g : 128 * (g + 1)]
            q8[:, 4 * s + g, :] = piece.astype(BF16).astype(F32)
        for i in range(2):
            piece = acc[rows, 512 + 128 * i : 640 + 128 * i].astype(BF16)
            new_kv[s, i] = piece
            kvn[s, i] = piece.astype(F32)
    locals_[5].wait()
    locals_[6].wait()
    scale = 1.0 / 128**0.5

    def attend(n):
        rows = pl.ds(16 * n, 16)
        q = q8[rows]
        score = lax.dot_general(
            q.astype(BF16), keys[rows], (((2,), (2,)), ((0,), (0,))), preferred_element_type=F32
        ) * scale
        slots = lax.broadcasted_iota(jnp.int32, (16, 8, 128), 2)
        score = jnp.where(slots < lens[rows][:, None, :], score, -1e30)
        own = [
            jnp.sum(q * kvn[t, 0, rows][:, None, :], axis=-1, keepdims=True) * scale
            for t in range(2)
        ]
        second = lax.broadcasted_iota(jnp.int32, (16, 8, 1), 1) >= 4
        own[1] = jnp.where(second, own[1], -1e30)
        top = jnp.maximum(jnp.max(score, axis=-1, keepdims=True), jnp.maximum(own[0], own[1]))
        cached = jnp.exp(score - top)
        fresh = [jnp.exp(o - top) for o in own]
        total = jnp.sum(cached, axis=-1, keepdims=True) + fresh[0] + fresh[1]
        weight = (cached / total).astype(BF16)
        result = lax.dot_general(
            weight, values[rows], (((2,), (1,)), ((0,), (0,))), preferred_element_type=F32
        )
        for t in range(2):
            w = (fresh[t] / total).astype(BF16).astype(F32)
            result = result + w * kvn[t, 1, rows][:, None, :]
        h8[rows] = result

    attend(0)
    attend(1)
    e2(1, 1)
    attend(2)
    attend(3)
    e3(1, 0)
    for s in range(2):
        for g in range(4):
            heads[64 * s : 64 * (s + 1), 128 * g : 128 * (g + 1)] = h8[:, 4 * s + g, :].astype(BF16)
    e3(1, 1)
    e2(1, 2)
    e3(1, 2)
    e2(1, 3)
    e3(1, 3)
    for k in range(4):
        e4(1, k)

    def product(j, t):
        right = wb[inverse[t * 4 + j]]
        part[j, t] = jnp.dot(heads[...], right, preferred_element_type=F32).astype(BF16)

    def r_send_to(j, i, src, dst, to):
        send(src, dst, r_send.at[j, i], r_recv.at[j, i], to)

    to_left, to_right = device(y_=yl), device(y_=yr)
    for j in range(4):
        product(j, yo * 2)
        r_send_to(j, 0, part.at[j, yo * 2], transit.at[j, 0], to_right)
        product(j, yo * 2 + 1)
        r_send_to(j, 1, part.at[j, yo * 2 + 1], transit.at[j, 1], to_left)
        product(j, yr * 2 + 1)
        r_send_to(j, 2, part.at[j, yr * 2 + 1], from_left.at[j, 1], to_right)
        product(j, yl * 2)
        r_send_to(j, 3, part.at[j, yl * 2], from_right.at[j, 0], to_left)
        product(j, yr * 2)
        product(j, yl * 2 + 1)
        product(j, y * 2)
        product(j, y * 2 + 1)

    def add(j, t, i):
        part[j, t] = (part[j, t].astype(F32) + transit[j, i].astype(F32)).astype(BF16)

    for j in range(4):
        arrived(transit.at[j, 0], r_recv.at[j, 0])
        add(j, yr * 2, 0)
        r_send_to(j, 4, part.at[j, yr * 2], from_left.at[j, 0], to_right)
        arrived(transit.at[j, 1], r_recv.at[j, 1])
        add(j, yl * 2 + 1, 1)
        r_send_to(j, 5, part.at[j, yl * 2 + 1], from_right.at[j, 1], to_left)

    def summed(j, h):
        return (
            part[j, y * 2 + h].astype(F32) + from_left[j, h].astype(F32) + from_right[j, h].astype(F32)
        )

    for j in range(4):
        arrived(from_left.at[j, 1], r_recv.at[j, 2])
        arrived(from_right.at[j, 0], r_recv.at[j, 3])
        arrived(from_left.at[j, 0], r_recv.at[j, 4])
        arrived(from_right.at[j, 1], r_recv.at[j, 5])
        far_out[j] = summed(j, 1 - zh).astype(BF16)
        r_send_to(j, 6, far_out.at[j], far_in.at[j], device(zh_=1 - zh))
    for j in range(4):
        arrived(far_in.at[j], r_recv.at[j, 6])
        out[:, 256 * j : 256 * (j + 1)] = (summed(j, zh) + far_in[j].astype(F32)).astype(BF16)

    for copy in sent:
        copy.wait_send()

    @pl.when(inner)
    def _():
        for copy in inner_sent:
            copy.wait_send()


def on_device(states, cache, lengths, plan, wq_new, wkv_new, wo_new):
    vmem = pltpu.VMEM
    dma = pltpu.SemaphoreType.DMA
    hbm = pl.BlockSpec(memory_space=pltpu.HBM)
    smem = pl.BlockSpec(memory_space=pltpu.SMEM)
    attended, new_kv = pl.pallas_call(
        kernel,
        out_shape=(
            jax.ShapeDtypeStruct((128, 1024), BF16),
            jax.ShapeDtypeStruct((2, 2, 64, 128), BF16),
        ),
        in_specs=[smem, smem, hbm, hbm, hbm, hbm, hbm],
        out_specs=[pl.BlockSpec(memory_space=pltpu.VMEM)] * 2,
        scratch_shapes=[
            vmem((256, 512), BF16),
            vmem((2, 256, 128), BF16),
            vmem((32, 256, 768), BF16),
            vmem((32, 512, 256), BF16),
            vmem((8, 128, 1024), BF16),
            vmem((32, 128, 256), BF16),
            vmem((128, 768), F32),
            vmem((64, 128, 128), BF16),
            vmem((64, 128, 128), BF16),
            vmem((64, 128), jnp.int32),
            vmem((64, 8, 128), F32),
            vmem((64, 8, 128), F32),
            vmem((128, 512), BF16),
            vmem((2, 2, 64, 128), F32),
            pltpu.SMEM((32,), jnp.int32),
            vmem((4, 8, 128, 256), BF16),
            vmem((4, 2, 128, 256), BF16),
            vmem((4, 2, 128, 256), BF16),
            vmem((4, 2, 128, 256), BF16),
            vmem((4, 128, 256), BF16),
            vmem((4, 128, 256), BF16),
            dma((7,)),
            dma((7,)), dma((7,)),
            dma((2, 35)), dma((2, 35)), dma((2, 4)),
            dma((4, 7)), dma((4, 7)),
        ],
        compiler_params=pltpu.CompilerParams(
            collective_id=0, has_side_effects=True, vmem_limit_bytes=60 * 2**20
        ),
        name="layer",
    )(
        plan, lengths, states.reshape(128, 1024), cache.reshape(2, 64, 128, 128),
        wq_new, wkv_new, wo_new,
    )
    return attended.reshape(2, 64, 1024), new_kv.reshape(2, 2, 64, 1, 128)


def solution(mesh):
    return jax.shard_map(
        on_device,
        mesh=mesh,
        in_specs=(
            P(None, "grp", "tp"),
            P(None, "grp", "tp", None, None),
            P("grp"),
            P(),
            P("grp", "tp"),
            P(None, "grp", "tp"),
            P("tp", "grp"),
        ),
        out_specs=(P(None, "grp", "tp"), P(None, None, "grp", "tp", None)),
        check_vma=False,
    )
```

```python
import functools

import jax
import jax.numpy as jnp
from jax import lax
from jax.experimental import pallas as pl
from jax.experimental.pallas import tpu as pltpu
from jax.sharding import PartitionSpec as P

MESH = pl.DeviceIdType.MESH
FIRST = 192
REST = 512 - FIRST
F32 = jnp.float32
BF16 = jnp.bfloat16


def kernel(
    plan, lengths, states, cache, wq, wkv, wo,
    out, new_kv,
    own_q, own_kv,
    wa0, wa1, wa2, wa3, wb, wc, st, xn, xp, acc, keys, values, lens, q8, h8, heads, kvn, inverse,
    part, from_left, from_right, transit, far_out, far_in,
    local_sem, st_send, st_recv, w_send, w_recv, z_send, c_send, c_recv, cz_send, r_send, r_recv,
):
    grp = lax.axis_index("grp")
    tp = lax.axis_index("tp")
    z, x, c = grp // 8, lax.rem(grp // 2, 4), lax.rem(grp, 2)
    y, zh = tp // 2, lax.rem(tp, 2)

    def mod4(v):
        return lax.rem(v + 4, 4)

    def block_of(z_, x_, c_):
        return (z_ * 4 + x_) * 2 + c_

    def device(x_=x, y_=y, z_=z, zh_=zh, c_=c):
        return (block_of(z_, x_, c_), y_ * 2 + zh_)

    xl, xr, xo = mod4(x - 1), mod4(x + 1), mod4(x + 2)
    yl, yr, yo = mod4(y - 1), mod4(y + 1), mod4(y + 2)
    z_pair, z_mirror = z + 1 - 2 * lax.rem(z, 2), 3 - z
    upper = z // 2
    inner = lax.rem(z + 1, 4) // 2 == 1
    zk = [z, z_pair, 2 - upper, 3 - 3 * upper]

    locals_ = [
        pltpu.make_async_copy(wq, own_q, local_sem.at[0]),
        pltpu.make_async_copy(wkv.at[0], own_kv.at[0], local_sem.at[1]),
        pltpu.make_async_copy(wkv.at[1], own_kv.at[1], local_sem.at[2]),
        pltpu.make_async_copy(states, st.at[tp], local_sem.at[3]),
        pltpu.make_async_copy(wo.at[pl.ds(FIRST, REST)], wb.at[grp], local_sem.at[4]),
        pltpu.make_async_copy(cache.at[0], keys, local_sem.at[5]),
        pltpu.make_async_copy(cache.at[1], values, local_sem.at[6]),
        pltpu.make_async_copy(wo.at[pl.ds(0, FIRST)], wc.at[c * 16 + z * 4 + x], local_sem.at[7]),
    ]
    for copy in locals_:
        copy.start()

    partners = [
        device(x_=xl), device(x_=xr), device(c_=1 - c),
        device(y_=yl), device(y_=yr), device(y_=yo), device(zh_=1 - zh),
        device(z_=z_pair), device(z_=z_mirror),
    ]
    barrier = pltpu.get_barrier_semaphore()
    for partner in partners:
        pl.semaphore_signal(barrier, inc=1, device_id=partner, device_id_type=MESH)
    for i in (0, 1, 2):
        locals_[i].wait()
    mine = x * 2 + c
    wa0[mine, :, 0:512] = own_q[...]
    wa0[mine, :, 512:640] = own_kv[0]
    wa0[mine, :, 640:768] = own_kv[1]
    pl.semaphore_wait(barrier, len(partners))

    sent = []

    def send(src, dst, send_sem, recv_sem, to):
        copy = pltpu.make_async_remote_copy(
            src_ref=src, dst_ref=dst, send_sem=send_sem, recv_sem=recv_sem,
            device_id=to, device_id_type=MESH,
        )
        copy.start()
        sent.append(copy)

    def arrived(dst, recv_sem):
        pltpu.make_async_remote_copy(
            src_ref=dst, dst_ref=dst, send_sem=recv_sem, recv_sem=recv_sem,
            device_id=device(c_=1 - c), device_id_type=MESH,
        ).wait_recv()

    wa = (wa0, wa1, wa2, wa3)

    def held(t, k, x_, c_, there=None):
        if t == 0:
            return wa[k if there is None else there].at[x_ * 2 + c_]
        return wb.at[block_of(zk[k], x_, c_)]

    halves = (128, REST // 2)

    def z_start(t):
        send(held(t, 0, x, c), held(t, 0, x, c, 1), w_send.at[t, 0], w_recv.at[t, 0], device(z_=z_pair))
        pl.when(inner)(lambda: z_copy(t, 0).start())

    def z_copy(t, k):
        there = k + 2 if k < 2 else k
        return pltpu.make_async_remote_copy(
            src_ref=held(t, k, x, c), dst_ref=held(t, k, x, c, there),
            send_sem=z_send.at[t, k], recv_sem=w_recv.at[t, there - 1],
            device_id=device(z_=z_mirror) if k < 2 else device(z_=z_pair), device_id_type=MESH,
        )

    def z_in(t, k):
        @pl.when(inner)
        def _():
            arrived(held(t, k, x, c), w_recv.at[t, k - 1])
            z_copy(t, k).start()

    def z_out(t, k):
        @pl.when(jnp.logical_not(inner))
        def _():
            arrived(held(t, k, x, c), w_recv.at[t, k - 1])

    def base(k):
        return 3 + 8 * k

    def sibling(t, k, i, ref):
        s = base(k) + 4 + i
        send(ref, ref, w_send.at[t, s], w_recv.at[t, s], device(c_=1 - c))

    def e1(t, k):
        ref = held(t, k, x, c)
        s = base(k)
        send(ref, ref, w_send.at[t, s], w_recv.at[t, s], device(x_=xr))
        send(ref, ref, w_send.at[t, s + 1], w_recv.at[t, s + 1], device(x_=xl))
        sibling(t, k, 0, ref)

    def e2(t, k):
        s = base(k)
        half = halves[t]
        for i, x_, to, rows in ((0, xl, xr, pl.ds(0, half)), (1, xr, xl, pl.ds(half, half))):
            ref = held(t, k, x_, c)
            arrived(ref, w_recv.at[t, s + i])
            part_ref = ref.at[rows]
            send(part_ref, part_ref, w_send.at[t, s + 2 + i], w_recv.at[t, s + 2 + i], device(x_=to))
            sibling(t, k, 1 + i, ref)

    def e3(t, k):
        s = base(k)
        half = halves[t]
        ref = held(t, k, xo, c)
        arrived(ref.at[pl.ds(0, half)], w_recv.at[t, s + 2])
        arrived(ref.at[pl.ds(half, half)], w_recv.at[t, s + 3])
        sibling(t, k, 3, ref)

    def e4(t, k):
        for i, x_ in enumerate((x, xl, xr, xo)):
            arrived(held(t, k, x_, 1 - c), w_recv.at[t, base(k) + 4 + i])

    def first_of(z_, x_, c_):
        return c_ * 16 + z_ * 4 + x_

    def first_row(k, c_):
        return wc.at[pl.ds(first_of(zk[k], 0, c_), 4)]

    def c1():
        ref = wc.at[first_of(z, x, c)]
        send(ref, ref, c_send.at[0], c_recv.at[0], device(x_=xr))
        send(ref, ref, c_send.at[1], c_recv.at[1], device(x_=xl))

    def c2():
        half = FIRST // 2
        for i, x_, to, rows in ((0, xl, xr, pl.ds(0, half)), (1, xr, xl, pl.ds(half, half))):
            n = first_of(z, x_, c)
            arrived(wc.at[n], c_recv.at[i])
            ref = wc.at[n, rows]
            send(ref, ref, c_send.at[2 + i], c_recv.at[2 + i], device(x_=to))

    def c_copy(k):
        ref = first_row(k, c)
        arrives = 5 + k if k < 2 else 3 + k
        return pltpu.make_async_remote_copy(
            src_ref=ref, dst_ref=ref, send_sem=cz_send.at[k], recv_sem=c_recv.at[arrives],
            device_id=device(z_=z_mirror) if k < 2 else device(z_=z_pair), device_id_type=MESH,
        )

    def c_sibling(k):
        ref = first_row(k, c)
        send(ref, ref, c_send.at[7 + k], c_recv.at[7 + k], device(c_=1 - c))

    def c3():
        half = FIRST // 2
        n = first_of(z, xo, c)
        arrived(wc.at[n, pl.ds(0, half)], c_recv.at[2])
        arrived(wc.at[n, pl.ds(half, half)], c_recv.at[3])
        ref = first_row(0, c)
        send(ref, ref, c_send.at[4], c_recv.at[4], device(z_=z_pair))
        pl.when(inner)(lambda: c_copy(0).start())
        c_sibling(0)

    def c_in(k):
        @pl.when(inner)
        def _():
            arrived(first_row(k, c), c_recv.at[3 + k])
            c_copy(k).start()

    def c_out(k):
        @pl.when(jnp.logical_not(inner))
        def _():
            arrived(first_row(k, c), c_recv.at[3 + k])

    def c4():
        for k in range(4):
            arrived(first_row(k, 1 - c), c_recv.at[7 + k])

    tp_far = y * 2 + 1 - zh

    def spread_states(first, t):
        for i, y_ in enumerate((yr, yl, yo)):
            send(st.at[t], st.at[t], st_send.at[first + i], st_recv.at[first + i], device(y_=y_))

    e1(0, 0)
    locals_[3].wait()
    send(st.at[tp], st.at[tp], st_send.at[0], st_recv.at[0], device(zh_=1 - zh))
    z_start(0)
    spread_states(1, tp)
    locals_[7].wait()
    c1()
    locals_[4].wait()
    e1(1, 0)


    def one_length(r, carry):
        lens[pl.ds(r, 1), :] = jnp.full((1, 128), lengths[r], jnp.int32)
        return carry

    lax.fori_loop(0, 64, one_length, 0)

    def one_inverse(tb, carry):
        def look(b, found):
            return jnp.maximum(found, jnp.where(plan[b] == tb, b, 0))

        inverse[tb] = lax.fori_loop(0, 32, look, jnp.int32(0), unroll=32)
        return carry

    def some_inverse(n):
        lax.fori_loop(8 * n, 8 * n + 8, one_inverse, 0)

    e2(0, 0)
    c2()
    e2(1, 0)
    z_in(0, 1)
    z_in(0, 2)
    z_out(0, 1)
    e1(0, 1)
    arrived(st.at[tp_far], st_recv.at[0])
    spread_states(4, tp_far)
    e3(0, 0)
    e3(1, 0)
    z_in(0, 3)
    z_out(0, 2)
    e1(0, 2)
    e2(0, 1)
    e3(0, 1)
    z_out(0, 3)
    z_start(1)
    e1(0, 3)
    z_in(1, 1)
    z_in(1, 2)
    e2(0, 2)
    z_in(1, 3)
    c3()
    z_out(1, 1)
    e1(1, 1)
    e3(0, 2)

    for first, zh_ in ((1, zh), (4, 1 - zh)):
        for i, y_ in enumerate((yl, yr, yo)):
            arrived(st.at[y_ * 2 + zh_], st_recv.at[first + i])

    def squares(t, total):
        wide = st[t].astype(F32)
        return total + jnp.sum(wide * wide, axis=-1, keepdims=True)

    total = lax.fori_loop(0, 8, squares, jnp.zeros((128, 1), F32))
    gain = lax.rsqrt(total / 8192.0 + 1e-05)

    def normalise(t, carry):
        for j in range(4):
            wide = st[t, :, 256 * j : 256 * (j + 1)].astype(F32)
            xn[t * 4 + j] = (wide * gain).astype(BF16)
        return carry

    lax.fori_loop(0, 8, normalise, 0)
    for k in range(4):
        for i in range(8):
            xp[k, :, 256 * i : 256 * (i + 1)] = xn[plan[zk[k] * 8 + i]]

    def project(k):
        e4(0, k)
        for n in range(3):
            cols = slice(256 * n, 256 * (n + 1))
            right = wa[k][:, :, cols].reshape(2048, 256)
            sums = jnp.dot(xp[k], right, preferred_element_type=F32)
            acc[:, cols] = sums if k == 0 else acc[:, cols] + sums

    project(0)
    project(1)
    z_out(1, 2)
    e1(1, 2)
    project(2)
    c_in(1)
    c_in(2)
    e2(0, 3)
    z_out(1, 3)
    e1(1, 3)
    c_out(1)
    c_sibling(1)
    e3(0, 3)
    project(3)

    for s in range(2):
        rows = slice(64 * s, 64 * (s + 1))
        for g in range(4):
            piece = acc[rows, 128 * g : 128 * (g + 1)]
            q8[:, 4 * s + g, :] = piece.astype(BF16).astype(F32)
        for i in range(2):
            piece = acc[rows, 512 + 128 * i : 640 + 128 * i].astype(BF16)
            new_kv[s, i] = piece
            kvn[s, i] = piece.astype(F32)
    locals_[5].wait()
    locals_[6].wait()
    scale = 1.0 / 128**0.5

    def attend(n):
        rows = pl.ds(16 * n, 16)
        q = q8[rows]
        score = lax.dot_general(
            q.astype(BF16), keys[rows], (((2,), (2,)), ((0,), (0,))), preferred_element_type=F32
        ) * scale
        slots = lax.broadcasted_iota(jnp.int32, (16, 8, 128), 2)
        score = jnp.where(slots < lens[rows][:, None, :], score, -1e30)
        own = [
            jnp.sum(q * kvn[t, 0, rows][:, None, :], axis=-1, keepdims=True) * scale
            for t in range(2)
        ]
        second = lax.broadcasted_iota(jnp.int32, (16, 8, 1), 1) >= 4
        own[1] = jnp.where(second, own[1], -1e30)
        top = jnp.maximum(jnp.max(score, axis=-1, keepdims=True), jnp.maximum(own[0], own[1]))
        cached = jnp.exp(score - top)
        fresh = [jnp.exp(o - top) for o in own]
        total = jnp.sum(cached, axis=-1, keepdims=True) + fresh[0] + fresh[1]
        weight = (cached / total).astype(BF16)
        result = lax.dot_general(
            weight, values[rows], (((2,), (1,)), ((0,), (0,))), preferred_element_type=F32
        )
        for t in range(2):
            w = (fresh[t] / total).astype(BF16).astype(F32)
            result = result + w * kvn[t, 1, rows][:, None, :]
        h8[rows] = result

    e2(1, 1)
    attend(0)
    attend(1)
    c_in(3)
    attend(2)
    e3(1, 1)
    c_out(2)
    c_sibling(2)
    attend(3)
    e2(1, 2)
    for s in range(2):
        for g in range(4):
            heads[64 * s : 64 * (s + 1), 128 * g : 128 * (g + 1)] = h8[:, 4 * s + g, :].astype(BF16)
    some_inverse(0)
    some_inverse(1)
    e3(1, 2)
    some_inverse(2)
    some_inverse(3)
    e2(1, 3)
    c_out(3)
    c_sibling(3)
    e3(1, 3)
    for k in range(4):
        e4(1, k)
    c4()

    def product(j, t):
        b = inverse[t * 4 + j]
        low = jnp.dot(heads[:, :FIRST], wc[lax.rem(b, 2) * 16 + b // 2], preferred_element_type=F32)
        high = jnp.dot(heads[:, FIRST:], wb[b], preferred_element_type=F32)
        part[j, t] = (low + high).astype(BF16)

    def r_send_to(j, i, src, dst, to):
        send(src, dst, r_send.at[j, i], r_recv.at[j, i], to)

    to_left, to_right = device(y_=yl), device(y_=yr)

    def r1(j):
        product(j, yo * 2)
        r_send_to(j, 0, part.at[j, yo * 2], transit.at[j, 0], to_right)
        product(j, yo * 2 + 1)
        r_send_to(j, 1, part.at[j, yo * 2 + 1], transit.at[j, 1], to_left)
        product(j, yr * 2 + 1)
        r_send_to(j, 2, part.at[j, yr * 2 + 1], from_left.at[j, 1], to_right)
        product(j, yl * 2)
        r_send_to(j, 3, part.at[j, yl * 2], from_right.at[j, 0], to_left)
        product(j, yr * 2)
        product(j, yl * 2 + 1)
        product(j, y * 2)
        product(j, y * 2 + 1)

    def add(j, t, i):
        part[j, t] = (part[j, t].astype(F32) + transit[j, i].astype(F32)).astype(BF16)

    def r2(j):
        arrived(transit.at[j, 0], r_recv.at[j, 0])
        add(j, yr * 2, 0)
        r_send_to(j, 4, part.at[j, yr * 2], from_left.at[j, 0], to_right)
        arrived(transit.at[j, 1], r_recv.at[j, 1])
        add(j, yl * 2 + 1, 1)
        r_send_to(j, 5, part.at[j, yl * 2 + 1], from_right.at[j, 1], to_left)

    def summed(j, h):
        return (
            part[j, y * 2 + h].astype(F32) + from_left[j, h].astype(F32) + from_right[j, h].astype(F32)
        )

    def r3(j):
        arrived(from_left.at[j, 1], r_recv.at[j, 2])
        arrived(from_right.at[j, 0], r_recv.at[j, 3])
        arrived(from_left.at[j, 0], r_recv.at[j, 4])
        arrived(from_right.at[j, 1], r_recv.at[j, 5])
        far_out[j] = summed(j, 1 - zh).astype(BF16)
        r_send_to(j, 6, far_out.at[j], far_in.at[j], device(zh_=1 - zh))

    r1(0)
    r1(1)
    r2(0)
    r1(2)
    r2(1)
    r3(0)
    r1(3)
    r2(2)
    r3(1)
    r2(3)
    r3(2)
    r3(3)
    for j in range(4):
        arrived(far_in.at[j], r_recv.at[j, 6])
        out[:, 256 * j : 256 * (j + 1)] = (summed(j, zh) + far_in[j].astype(F32)).astype(BF16)

    for copy in sent:
        copy.wait_send()

    @pl.when(inner)
    def _():
        for k in range(4):
            for t in range(2):
                z_copy(t, k).wait_send()
            c_copy(k).wait_send()


def on_device(states, cache, lengths, plan, wq_new, wkv_new, wo_new):
    vmem = pltpu.VMEM
    dma = pltpu.SemaphoreType.DMA
    hbm = pl.BlockSpec(memory_space=pltpu.HBM)
    smem = pl.BlockSpec(memory_space=pltpu.SMEM)
    attended, new_kv = pl.pallas_call(
        kernel,
        out_shape=(
            jax.ShapeDtypeStruct((128, 1024), BF16),
            jax.ShapeDtypeStruct((2, 2, 64, 128), BF16),
        ),
        in_specs=[smem, smem, hbm, hbm, hbm, hbm, hbm],
        out_specs=[pl.BlockSpec(memory_space=pltpu.VMEM)] * 2,
        scratch_shapes=[
            vmem((256, 512), BF16),
            vmem((2, 256, 128), BF16),
            *[vmem((8, 256, 768), BF16)] * 4,
            vmem((32, REST, 256), BF16),
            vmem((32, FIRST, 256), BF16),
            vmem((8, 128, 1024), BF16),
            vmem((32, 128, 256), BF16),
            vmem((4, 128, 2048), BF16),
            vmem((128, 768), F32),
            vmem((64, 128, 128), BF16),
            vmem((64, 128, 128), BF16),
            vmem((64, 128), jnp.int32),
            vmem((64, 8, 128), F32),
            vmem((64, 8, 128), F32),
            vmem((128, 512), BF16),
            vmem((2, 2, 64, 128), F32),
            pltpu.SMEM((32,), jnp.int32),
            vmem((4, 8, 128, 256), BF16),
            vmem((4, 2, 128, 256), BF16),
            vmem((4, 2, 128, 256), BF16),
            vmem((4, 2, 128, 256), BF16),
            vmem((4, 128, 256), BF16),
            vmem((4, 128, 256), BF16),
            dma((8,)),
            dma((7,)), dma((7,)),
            dma((2, 35)), dma((2, 35)), dma((2, 4)),
            dma((11,)), dma((11,)), dma((4,)),
            dma((4, 7)), dma((4, 7)),
        ],
        compiler_params=pltpu.CompilerParams(
            collective_id=0, has_side_effects=True, vmem_limit_bytes=60 * 2**20
        ),
        name="layer",
    )(
        plan, lengths, states.reshape(128, 1024), cache.reshape(2, 64, 128, 128),
        wq_new, wkv_new, wo_new,
    )
    return attended.reshape(2, 64, 1024), new_kv.reshape(2, 2, 64, 1, 128)


def solution(mesh):
    return jax.shard_map(
        on_device,
        mesh=mesh,
        in_specs=(
            P(None, "grp", "tp"),
            P(None, "grp", "tp", None, None),
            P("grp"),
            P(),
            P("grp", "tp"),
            P(None, "grp", "tp"),
            P("tp", "grp"),
        ),
        out_specs=(P(None, "grp", "tp"), P(None, None, "grp", "tp", None)),
        check_vma=False,
    )
```

```python
import functools

import jax
import jax.numpy as jnp
from jax import lax
from jax.experimental import pallas as pl
from jax.experimental.pallas import tpu as pltpu
from jax.sharding import PartitionSpec as P

MESH = pl.DeviceIdType.MESH
FIRST = 192
REST = 512 - FIRST
F32 = jnp.float32
BF16 = jnp.bfloat16


def kernel(
    plan, lengths, states, cache, wq, wkv, wo,
    out, new_kv,
    own_q, own_kv,
    wa0, wa1, wa2, wa3, wb, wc, st, xn, xp, acc, keys, values, lens, q8, h8, heads, kvn, inverse,
    part, from_left, from_right, transit, far_out, far_in,
    local_sem, st_send, st_recv, w_send, w_recv, z_send, c_send, c_recv, cz_send, r_send, r_recv,
):
    grp = lax.axis_index("grp")
    tp = lax.axis_index("tp")
    z, x, c = grp // 8, lax.rem(grp // 2, 4), lax.rem(grp, 2)
    y, zh = tp // 2, lax.rem(tp, 2)

    def mod4(v):
        return lax.rem(v + 4, 4)

    def block_of(z_, x_, c_):
        return (z_ * 4 + x_) * 2 + c_

    def device(x_=x, y_=y, z_=z, zh_=zh, c_=c):
        return (block_of(z_, x_, c_), y_ * 2 + zh_)

    xl, xr, xo = mod4(x - 1), mod4(x + 1), mod4(x + 2)
    yl, yr, yo = mod4(y - 1), mod4(y + 1), mod4(y + 2)
    z_pair, z_mirror = z + 1 - 2 * lax.rem(z, 2), 3 - z
    upper = z // 2
    inner = lax.rem(z + 1, 4) // 2 == 1
    zk = [z, z_pair, 2 - upper, 3 - 3 * upper]

    locals_ = [
        pltpu.make_async_copy(wq, own_q, local_sem.at[0]),
        pltpu.make_async_copy(wkv.at[0], own_kv.at[0], local_sem.at[1]),
        pltpu.make_async_copy(wkv.at[1], own_kv.at[1], local_sem.at[2]),
        pltpu.make_async_copy(states, st.at[tp], local_sem.at[3]),
        pltpu.make_async_copy(wo.at[pl.ds(FIRST, REST)], wb.at[grp], local_sem.at[4]),
        pltpu.make_async_copy(cache.at[0], keys, local_sem.at[5]),
        pltpu.make_async_copy(cache.at[1], values, local_sem.at[6]),
        pltpu.make_async_copy(wo.at[pl.ds(0, FIRST)], wc.at[c * 16 + z * 4 + x], local_sem.at[7]),
    ]
    for copy in locals_:
        copy.start()

    partners = [
        device(x_=xl), device(x_=xr), device(c_=1 - c),
        device(y_=yl), device(y_=yr), device(y_=yo), device(zh_=1 - zh),
        device(z_=z_pair), device(z_=z_mirror),
    ]
    barrier = pltpu.get_barrier_semaphore()
    for partner in partners:
        pl.semaphore_signal(barrier, inc=1, device_id=partner, device_id_type=MESH)
    for i in (0, 1, 2):
        locals_[i].wait()
    mine = x * 2 + c
    wa0[mine, :, 0:512] = own_q[...]
    wa0[mine, :, 512:640] = own_kv[0]
    wa0[mine, :, 640:768] = own_kv[1]
    pl.semaphore_wait(barrier, len(partners))

    sent = []

    def send(src, dst, send_sem, recv_sem, to):
        copy = pltpu.make_async_remote_copy(
            src_ref=src, dst_ref=dst, send_sem=send_sem, recv_sem=recv_sem,
            device_id=to, device_id_type=MESH,
        )
        copy.start()
        sent.append(copy)

    def arrived(dst, recv_sem):
        pltpu.make_async_remote_copy(
            src_ref=dst, dst_ref=dst, send_sem=recv_sem, recv_sem=recv_sem,
            device_id=device(c_=1 - c), device_id_type=MESH,
        ).wait_recv()

    wa = (wa0, wa1, wa2, wa3)

    def held(t, k, x_, c_, there=None):
        if t == 0:
            return wa[k if there is None else there].at[x_ * 2 + c_]
        return wb.at[block_of(zk[k], x_, c_)]

    halves = (128, REST // 2)

    def z_start(t):
        send(held(t, 0, x, c), held(t, 0, x, c, 1), w_send.at[t, 0], w_recv.at[t, 0], device(z_=z_pair))
        pl.when(inner)(lambda: z_copy(t, 0).start())

    def z_copy(t, k):
        there = k + 2 if k < 2 else k
        return pltpu.make_async_remote_copy(
            src_ref=held(t, k, x, c), dst_ref=held(t, k, x, c, there),
            send_sem=z_send.at[t, k], recv_sem=w_recv.at[t, there - 1],
            device_id=device(z_=z_mirror) if k < 2 else device(z_=z_pair), device_id_type=MESH,
        )

    def z_in(t, k):
        @pl.when(inner)
        def _():
            arrived(held(t, k, x, c), w_recv.at[t, k - 1])
            z_copy(t, k).start()

    def z_out(t, k):
        @pl.when(jnp.logical_not(inner))
        def _():
            arrived(held(t, k, x, c), w_recv.at[t, k - 1])

    def base(k):
        return 3 + 8 * k

    def sibling(t, k, i, ref):
        s = base(k) + 4 + i
        send(ref, ref, w_send.at[t, s], w_recv.at[t, s], device(c_=1 - c))

    def e1(t, k):
        ref = held(t, k, x, c)
        s = base(k)
        send(ref, ref, w_send.at[t, s], w_recv.at[t, s], device(x_=xr))
        send(ref, ref, w_send.at[t, s + 1], w_recv.at[t, s + 1], device(x_=xl))
        sibling(t, k, 0, ref)

    def e2(t, k):
        s = base(k)
        half = halves[t]
        for i, x_, to, rows in ((0, xl, xr, pl.ds(0, half)), (1, xr, xl, pl.ds(half, half))):
            ref = held(t, k, x_, c)
            arrived(ref, w_recv.at[t, s + i])
            part_ref = ref.at[rows]
            send(part_ref, part_ref, w_send.at[t, s + 2 + i], w_recv.at[t, s + 2 + i], device(x_=to))
            sibling(t, k, 1 + i, ref)

    def e3(t, k):
        s = base(k)
        half = halves[t]
        ref = held(t, k, xo, c)
        arrived(ref.at[pl.ds(0, half)], w_recv.at[t, s + 2])
        arrived(ref.at[pl.ds(half, half)], w_recv.at[t, s + 3])
        sibling(t, k, 3, ref)

    def e4(t, k):
        for i, x_ in enumerate((x, xl, xr, xo)):
            arrived(held(t, k, x_, 1 - c), w_recv.at[t, base(k) + 4 + i])

    def first_of(z_, x_, c_):
        return c_ * 16 + z_ * 4 + x_

    def first_row(k, c_):
        return wc.at[pl.ds(first_of(zk[k], 0, c_), 4)]

    def c1():
        ref = wc.at[first_of(z, x, c)]
        send(ref, ref, c_send.at[0], c_recv.at[0], device(x_=xr))
        send(ref, ref, c_send.at[1], c_recv.at[1], device(x_=xl))

    def c2():
        half = FIRST // 2
        for i, x_, to, rows in ((0, xl, xr, pl.ds(0, half)), (1, xr, xl, pl.ds(half, half))):
            n = first_of(z, x_, c)
            arrived(wc.at[n], c_recv.at[i])
            ref = wc.at[n, rows]
            send(ref, ref, c_send.at[2 + i], c_recv.at[2 + i], device(x_=to))

    def c_copy(k):
        ref = first_row(k, c)
        arrives = 5 + k if k < 2 else 3 + k
        return pltpu.make_async_remote_copy(
            src_ref=ref, dst_ref=ref, send_sem=cz_send.at[k], recv_sem=c_recv.at[arrives],
            device_id=device(z_=z_mirror) if k < 2 else device(z_=z_pair), device_id_type=MESH,
        )

    def c_sibling(k):
        ref = first_row(k, c)
        send(ref, ref, c_send.at[7 + k], c_recv.at[7 + k], device(c_=1 - c))

    def c3():
        half = FIRST // 2
        n = first_of(z, xo, c)
        arrived(wc.at[n, pl.ds(0, half)], c_recv.at[2])
        arrived(wc.at[n, pl.ds(half, half)], c_recv.at[3])
        ref = first_row(0, c)
        send(ref, ref, c_send.at[4], c_recv.at[4], device(z_=z_pair))
        pl.when(inner)(lambda: c_copy(0).start())
        c_sibling(0)

    def c_in(k):
        @pl.when(inner)
        def _():
            arrived(first_row(k, c), c_recv.at[3 + k])
            c_copy(k).start()

    def c_out(k):
        @pl.when(jnp.logical_not(inner))
        def _():
            arrived(first_row(k, c), c_recv.at[3 + k])

    def c4():
        for k in range(4):
            arrived(first_row(k, 1 - c), c_recv.at[7 + k])

    tp_far = y * 2 + 1 - zh

    def spread_states(first, t):
        for i, y_ in enumerate((yr, yl, yo)):
            send(st.at[t], st.at[t], st_send.at[first + i], st_recv.at[first + i], device(y_=y_))

    e1(0, 0)
    locals_[3].wait()
    send(st.at[tp], st.at[tp], st_send.at[0], st_recv.at[0], device(zh_=1 - zh))
    z_start(0)
    spread_states(1, tp)
    locals_[7].wait()
    c1()
    locals_[4].wait()
    e1(1, 0)


    def one_length(r, carry):
        lens[pl.ds(r, 1), :] = jnp.full((1, 128), lengths[r], jnp.int32)
        return carry

    lax.fori_loop(0, 64, one_length, 0)

    def one_inverse(tb, carry):
        def look(b, found):
            return jnp.maximum(found, jnp.where(plan[b] == tb, b, 0))

        inverse[tb] = lax.fori_loop(0, 32, look, jnp.int32(0), unroll=32)
        return carry

    def some_inverse(n):
        lax.fori_loop(8 * n, 8 * n + 8, one_inverse, 0)

    e2(0, 0)
    c2()
    e2(1, 0)
    z_in(0, 1)
    z_in(0, 2)
    z_out(0, 1)
    e1(0, 1)
    arrived(st.at[tp_far], st_recv.at[0])
    spread_states(4, tp_far)
    e3(0, 0)
    e3(1, 0)
    z_in(0, 3)
    z_out(0, 2)
    e1(0, 2)
    e2(0, 1)
    e3(0, 1)
    z_out(0, 3)
    z_start(1)
    e1(0, 3)
    z_in(1, 1)
    z_in(1, 2)
    e2(0, 2)
    z_in(1, 3)
    c3()
    z_out(1, 1)
    e1(1, 1)
    e3(0, 2)
    z_out(1, 2)
    e1(1, 2)

    for first, zh_ in ((1, zh), (4, 1 - zh)):
        for i, y_ in enumerate((yl, yr, yo)):
            arrived(st.at[y_ * 2 + zh_], st_recv.at[first + i])

    def squares(t, total):
        wide = st[t].astype(F32)
        return total + jnp.sum(wide * wide, axis=-1, keepdims=True)

    total = lax.fori_loop(0, 8, squares, jnp.zeros((128, 1), F32))
    gain = lax.rsqrt(total / 8192.0 + 1e-05)

    def normalise(t, carry):
        for j in range(4):
            wide = st[t, :, 256 * j : 256 * (j + 1)].astype(F32)
            xn[t * 4 + j] = (wide * gain).astype(BF16)
        return carry

    lax.fori_loop(0, 8, normalise, 0)
    for k in range(4):
        for i in range(8):
            xp[k, :, 256 * i : 256 * (i + 1)] = xn[plan[zk[k] * 8 + i]]

    def project(k):
        e4(0, k)
        for n in range(3):
            cols = slice(256 * n, 256 * (n + 1))
            right = wa[k][:, :, cols].reshape(2048, 256)
            sums = jnp.dot(xp[k], right, preferred_element_type=F32)
            acc[:, cols] = sums if k == 0 else acc[:, cols] + sums

    project(0)
    project(1)
    project(2)
    c_in(1)
    c_in(2)
    e2(0, 3)
    z_out(1, 3)
    e1(1, 3)
    c_out(1)
    c_sibling(1)
    e3(0, 3)
    project(3)

    for s in range(2):
        rows = slice(64 * s, 64 * (s + 1))
        for g in range(4):
            piece = acc[rows, 128 * g : 128 * (g + 1)]
            q8[:, 4 * s + g, :] = piece.astype(BF16).astype(F32)
        for i in range(2):
            piece = acc[rows, 512 + 128 * i : 640 + 128 * i].astype(BF16)
            new_kv[s, i] = piece
            kvn[s, i] = piece.astype(F32)
    locals_[5].wait()
    locals_[6].wait()
    scale = 1.0 / 128**0.5

    def attend(n):
        rows = pl.ds(16 * n, 16)
        q = q8[rows]
        score = lax.dot_general(
            q.astype(BF16), keys[rows], (((2,), (2,)), ((0,), (0,))), preferred_element_type=F32
        ) * scale
        slots = lax.broadcasted_iota(jnp.int32, (16, 8, 128), 2)
        score = jnp.where(slots < lens[rows][:, None, :], score, -1e30)
        own = [
            jnp.sum(q * kvn[t, 0, rows][:, None, :], axis=-1, keepdims=True) * scale
            for t in range(2)
        ]
        second = lax.broadcasted_iota(jnp.int32, (16, 8, 1), 1) >= 4
        own[1] = jnp.where(second, own[1], -1e30)
        top = jnp.maximum(jnp.max(score, axis=-1, keepdims=True), jnp.maximum(own[0], own[1]))
        cached = jnp.exp(score - top)
        fresh = [jnp.exp(o - top) for o in own]
        total = jnp.sum(cached, axis=-1, keepdims=True) + fresh[0] + fresh[1]
        weight = (cached / total).astype(BF16)
        result = lax.dot_general(
            weight, values[rows], (((2,), (1,)), ((0,), (0,))), preferred_element_type=F32
        )
        for t in range(2):
            w = (fresh[t] / total).astype(BF16).astype(F32)
            result = result + w * kvn[t, 1, rows][:, None, :]
        h8[rows] = result

    e2(1, 1)
    attend(0)
    attend(1)
    c_in(3)
    e2(1, 2)
    attend(2)
    e3(1, 1)
    c_out(2)
    c_sibling(2)
    attend(3)

    for s in range(2):
        for g in range(4):
            heads[64 * s : 64 * (s + 1), 128 * g : 128 * (g + 1)] = h8[:, 4 * s + g, :].astype(BF16)
    some_inverse(0)
    e3(1, 2)
    some_inverse(1)
    e2(1, 3)
    some_inverse(2)
    some_inverse(3)
    c_out(3)
    c_sibling(3)
    e3(1, 3)

    for k in range(4):
        e4(1, k)
    c4()

    def product(j, t):
        b = inverse[t * 4 + j]
        low = jnp.dot(heads[:, :FIRST], wc[lax.rem(b, 2) * 16 + b // 2], preferred_element_type=F32)
        high = jnp.dot(heads[:, FIRST:], wb[b], preferred_element_type=F32)
        part[j, t] = (low + high).astype(BF16)

    def r_send_to(j, i, src, dst, to):
        send(src, dst, r_send.at[j, i], r_recv.at[j, i], to)

    to_left, to_right = device(y_=yl), device(y_=yr)

    def r1(j):
        product(j, yo * 2)
        r_send_to(j, 0, part.at[j, yo * 2], transit.at[j, 0], to_right)
        product(j, yo * 2 + 1)
        r_send_to(j, 1, part.at[j, yo * 2 + 1], transit.at[j, 1], to_left)
        product(j, yr * 2 + 1)
        r_send_to(j, 2, part.at[j, yr * 2 + 1], from_left.at[j, 1], to_right)
        product(j, yl * 2)
        r_send_to(j, 3, part.at[j, yl * 2], from_right.at[j, 0], to_left)
        product(j, yr * 2)
        product(j, yl * 2 + 1)
        product(j, y * 2)
        product(j, y * 2 + 1)

    def add(j, t, i):
        part[j, t] = (part[j, t].astype(F32) + transit[j, i].astype(F32)).astype(BF16)

    def r2(j):
        arrived(transit.at[j, 0], r_recv.at[j, 0])
        add(j, yr * 2, 0)
        r_send_to(j, 4, part.at[j, yr * 2], from_left.at[j, 0], to_right)
        arrived(transit.at[j, 1], r_recv.at[j, 1])
        add(j, yl * 2 + 1, 1)
        r_send_to(j, 5, part.at[j, yl * 2 + 1], from_right.at[j, 1], to_left)

    def summed(j, h):
        return (
            part[j, y * 2 + h].astype(F32) + from_left[j, h].astype(F32) + from_right[j, h].astype(F32)
        )

    def r3(j):
        arrived(from_left.at[j, 1], r_recv.at[j, 2])
        arrived(from_right.at[j, 0], r_recv.at[j, 3])
        arrived(from_left.at[j, 0], r_recv.at[j, 4])
        arrived(from_right.at[j, 1], r_recv.at[j, 5])
        far_out[j] = summed(j, 1 - zh).astype(BF16)
        r_send_to(j, 6, far_out.at[j], far_in.at[j], device(zh_=1 - zh))

    r1(0)
    r1(1)
    r2(0)
    r1(2)
    r2(1)
    r3(0)
    r1(3)
    r2(2)
    r3(1)
    r2(3)
    r3(2)
    r3(3)
    for j in range(4):
        arrived(far_in.at[j], r_recv.at[j, 6])
        out[:, 256 * j : 256 * (j + 1)] = (summed(j, zh) + far_in[j].astype(F32)).astype(BF16)

    for copy in sent:
        copy.wait_send()

    @pl.when(inner)
    def _():
        for k in range(4):
            for t in range(2):
                z_copy(t, k).wait_send()
            c_copy(k).wait_send()


def finish(sums, fresh, out, new_kv):
    out[...] = sums[...]
    new_kv[...] = fresh[...]


def on_device(states, cache, lengths, plan, wq_new, wkv_new, wo_new):
    vmem = pltpu.VMEM
    dma = pltpu.SemaphoreType.DMA
    hbm = pl.BlockSpec(memory_space=pltpu.HBM)
    smem = pl.BlockSpec(memory_space=pltpu.SMEM)
    attended, new_kv = pl.pallas_call(
        kernel,
        out_shape=(
            jax.ShapeDtypeStruct((128, 1024), BF16),
            jax.ShapeDtypeStruct((2, 2, 64, 128), BF16),
        ),
        in_specs=[smem, smem, hbm, hbm, hbm, hbm, hbm],
        out_specs=[pl.BlockSpec(memory_space=pltpu.VMEM)] * 2,
        scratch_shapes=[
            vmem((256, 512), BF16),
            vmem((2, 256, 128), BF16),
            *[vmem((8, 256, 768), BF16)] * 4,
            vmem((32, REST, 256), BF16),
            vmem((32, FIRST, 256), BF16),
            vmem((8, 128, 1024), BF16),
            vmem((32, 128, 256), BF16),
            vmem((4, 128, 2048), BF16),
            vmem((128, 768), F32),
            vmem((64, 128, 128), BF16),
            vmem((64, 128, 128), BF16),
            vmem((64, 128), jnp.int32),
            vmem((64, 8, 128), F32),
            vmem((64, 8, 128), F32),
            vmem((128, 512), BF16),
            vmem((2, 2, 64, 128), F32),
            pltpu.SMEM((32,), jnp.int32),
            vmem((4, 8, 128, 256), BF16),
            vmem((4, 2, 128, 256), BF16),
            vmem((4, 2, 128, 256), BF16),
            vmem((4, 2, 128, 256), BF16),
            vmem((4, 128, 256), BF16),
            vmem((4, 128, 256), BF16),
            dma((8,)),
            dma((7,)), dma((7,)),
            dma((2, 35)), dma((2, 35)), dma((2, 4)),
            dma((11,)), dma((11,)), dma((4,)),
            dma((4, 7)), dma((4, 7)),
        ],
        compiler_params=pltpu.CompilerParams(
            collective_id=0, has_side_effects=True, vmem_limit_bytes=60 * 2**20
        ),
        name="layer",
    )(
        plan, lengths, states.reshape(128, 1024), cache.reshape(2, 64, 128, 128),
        wq_new, wkv_new, wo_new,
    )
    whole = pl.BlockSpec(memory_space=pltpu.VMEM)
    attended, new_kv = pl.pallas_call(
        finish,
        out_shape=(
            jax.ShapeDtypeStruct((128, 1024), BF16),
            jax.ShapeDtypeStruct((2, 2, 64, 128), BF16),
        ),
        in_specs=[whole, whole],
        out_specs=[whole, whole],
        name="finish",
    )(attended, new_kv)
    return attended.reshape(2, 64, 1024), new_kv.reshape(2, 2, 64, 1, 128)


def solution(mesh):
    return jax.shard_map(
        on_device,
        mesh=mesh,
        in_specs=(
            P(None, "grp", "tp"),
            P(None, "grp", "tp", None, None),
            P("grp"),
            P(),
            P("grp", "tp"),
            P(None, "grp", "tp"),
            P("tp", "grp"),
        ),
        out_specs=(P(None, "grp", "tp"), P(None, None, "grp", "tp", None)),
        check_vma=False,
    )
```

```python
import functools

import jax
import jax.numpy as jnp
from jax import lax
from jax.experimental import pallas as pl
from jax.experimental.pallas import tpu as pltpu
from jax.sharding import PartitionSpec as P

MESH = pl.DeviceIdType.MESH
FIRST = 192
REST = 512 - FIRST
F32 = jnp.float32
BF16 = jnp.bfloat16


def kernel(
    plan, lengths, states, cache, wq, wkv, wo,
    out, new_kv,
    own_q, own_kv,
    wa0, wa1, wa2, wa3, wb, wc, st, xn, xp, acc, keys, values, lens, q8, h8, heads, kvn, inverse,
    part, from_left, from_right, transit, far_out, far_in, mine_sum,
    local_sem, st_send, st_recv, w_send, w_recv, z_send, c_send, c_recv, cz_send, r_send, r_recv,
):
    grp = lax.axis_index("grp")
    tp = lax.axis_index("tp")
    z, x, c = grp // 8, lax.rem(grp // 2, 4), lax.rem(grp, 2)
    y, zh = tp // 2, lax.rem(tp, 2)

    def mod4(v):
        return lax.rem(v + 4, 4)

    def block_of(z_, x_, c_):
        return (z_ * 4 + x_) * 2 + c_

    def device(x_=x, y_=y, z_=z, zh_=zh, c_=c):
        return (block_of(z_, x_, c_), y_ * 2 + zh_)

    xl, xr, xo = mod4(x - 1), mod4(x + 1), mod4(x + 2)
    yl, yr, yo = mod4(y - 1), mod4(y + 1), mod4(y + 2)
    z_pair, z_mirror = z + 1 - 2 * lax.rem(z, 2), 3 - z
    upper = z // 2
    inner = lax.rem(z + 1, 4) // 2 == 1
    zk = [z, z_pair, 2 - upper, 3 - 3 * upper]

    locals_ = [
        pltpu.make_async_copy(wq, own_q, local_sem.at[0]),
        pltpu.make_async_copy(wkv.at[0], own_kv.at[0], local_sem.at[1]),
        pltpu.make_async_copy(wkv.at[1], own_kv.at[1], local_sem.at[2]),
        pltpu.make_async_copy(states, st.at[tp], local_sem.at[3]),
        pltpu.make_async_copy(wo.at[pl.ds(FIRST, REST)], wb.at[grp], local_sem.at[4]),
        pltpu.make_async_copy(cache.at[0], keys, local_sem.at[5]),
        pltpu.make_async_copy(cache.at[1], values, local_sem.at[6]),
        pltpu.make_async_copy(wo.at[pl.ds(0, FIRST)], wc.at[c * 16 + z * 4 + x], local_sem.at[7]),
    ]
    for copy in locals_:
        copy.start()

    partners = [
        device(x_=xl), device(x_=xr), device(c_=1 - c),
        device(y_=yl), device(y_=yr), device(y_=yo), device(zh_=1 - zh),
        device(z_=z_pair), device(z_=z_mirror),
    ]
    barrier = pltpu.get_barrier_semaphore()
    for partner in partners:
        pl.semaphore_signal(barrier, inc=1, device_id=partner, device_id_type=MESH)
    for i in (0, 1, 2):
        locals_[i].wait()
    mine = x * 2 + c
    wa0[mine, :, 0:512] = own_q[...]
    wa0[mine, :, 512:640] = own_kv[0]
    wa0[mine, :, 640:768] = own_kv[1]
    pl.semaphore_wait(barrier, len(partners))

    sent = []

    def send(src, dst, send_sem, recv_sem, to):
        copy = pltpu.make_async_remote_copy(
            src_ref=src, dst_ref=dst, send_sem=send_sem, recv_sem=recv_sem,
            device_id=to, device_id_type=MESH,
        )
        copy.start()
        sent.append(copy)

    def arrived(dst, recv_sem):
        pltpu.make_async_remote_copy(
            src_ref=dst, dst_ref=dst, send_sem=recv_sem, recv_sem=recv_sem,
            device_id=device(c_=1 - c), device_id_type=MESH,
        ).wait_recv()

    wa = (wa0, wa1, wa2, wa3)

    def held(t, k, x_, c_, there=None):
        if t == 0:
            return wa[k if there is None else there].at[x_ * 2 + c_]
        return wb.at[block_of(zk[k], x_, c_)]

    halves = (128, REST // 2)

    def z_start(t):
        send(held(t, 0, x, c), held(t, 0, x, c, 1), w_send.at[t, 0], w_recv.at[t, 0], device(z_=z_pair))
        pl.when(inner)(lambda: z_copy(t, 0).start())

    def z_copy(t, k):
        there = k + 2 if k < 2 else k
        return pltpu.make_async_remote_copy(
            src_ref=held(t, k, x, c), dst_ref=held(t, k, x, c, there),
            send_sem=z_send.at[t, k], recv_sem=w_recv.at[t, there - 1],
            device_id=device(z_=z_mirror) if k < 2 else device(z_=z_pair), device_id_type=MESH,
        )

    def z_in(t, k):
        @pl.when(inner)
        def _():
            arrived(held(t, k, x, c), w_recv.at[t, k - 1])
            z_copy(t, k).start()

    def z_out(t, k):
        @pl.when(jnp.logical_not(inner))
        def _():
            arrived(held(t, k, x, c), w_recv.at[t, k - 1])

    def base(k):
        return 3 + 8 * k

    def sibling(t, k, i, ref):
        s = base(k) + 4 + i
        send(ref, ref, w_send.at[t, s], w_recv.at[t, s], device(c_=1 - c))

    def e1(t, k):
        ref = held(t, k, x, c)
        s = base(k)
        send(ref, ref, w_send.at[t, s], w_recv.at[t, s], device(x_=xr))
        send(ref, ref, w_send.at[t, s + 1], w_recv.at[t, s + 1], device(x_=xl))
        sibling(t, k, 0, ref)

    def e2(t, k):
        s = base(k)
        half = halves[t]
        for i, x_, to, rows in ((0, xl, xr, pl.ds(0, half)), (1, xr, xl, pl.ds(half, half))):
            ref = held(t, k, x_, c)
            arrived(ref, w_recv.at[t, s + i])
            part_ref = ref.at[rows]
            send(part_ref, part_ref, w_send.at[t, s + 2 + i], w_recv.at[t, s + 2 + i], device(x_=to))
            sibling(t, k, 1 + i, ref)

    def e3(t, k):
        s = base(k)
        half = halves[t]
        ref = held(t, k, xo, c)
        arrived(ref.at[pl.ds(0, half)], w_recv.at[t, s + 2])
        arrived(ref.at[pl.ds(half, half)], w_recv.at[t, s + 3])
        sibling(t, k, 3, ref)

    def e4(t, k):
        for i, x_ in enumerate((x, xl, xr, xo)):
            arrived(held(t, k, x_, 1 - c), w_recv.at[t, base(k) + 4 + i])

    def first_of(z_, x_, c_):
        return c_ * 16 + z_ * 4 + x_

    def first_row(k, c_):
        return wc.at[pl.ds(first_of(zk[k], 0, c_), 4)]

    def c1():
        ref = wc.at[first_of(z, x, c)]
        send(ref, ref, c_send.at[0], c_recv.at[0], device(x_=xr))
        send(ref, ref, c_send.at[1], c_recv.at[1], device(x_=xl))

    def c2():
        half = FIRST // 2
        for i, x_, to, rows in ((0, xl, xr, pl.ds(0, half)), (1, xr, xl, pl.ds(half, half))):
            n = first_of(z, x_, c)
            arrived(wc.at[n], c_recv.at[i])
            ref = wc.at[n, rows]
            send(ref, ref, c_send.at[2 + i], c_recv.at[2 + i], device(x_=to))

    def c_copy(k):
        ref = first_row(k, c)
        arrives = 5 + k if k < 2 else 3 + k
        return pltpu.make_async_remote_copy(
            src_ref=ref, dst_ref=ref, send_sem=cz_send.at[k], recv_sem=c_recv.at[arrives],
            device_id=device(z_=z_mirror) if k < 2 else device(z_=z_pair), device_id_type=MESH,
        )

    def c_sibling(k):
        ref = first_row(k, c)
        send(ref, ref, c_send.at[7 + k], c_recv.at[7 + k], device(c_=1 - c))

    def c3():
        half = FIRST // 2
        n = first_of(z, xo, c)
        arrived(wc.at[n, pl.ds(0, half)], c_recv.at[2])
        arrived(wc.at[n, pl.ds(half, half)], c_recv.at[3])
        ref = first_row(0, c)
        send(ref, ref, c_send.at[4], c_recv.at[4], device(z_=z_pair))
        pl.when(inner)(lambda: c_copy(0).start())
        c_sibling(0)

    def c_in(k):
        @pl.when(inner)
        def _():
            arrived(first_row(k, c), c_recv.at[3 + k])
            c_copy(k).start()

    def c_out(k):
        @pl.when(jnp.logical_not(inner))
        def _():
            arrived(first_row(k, c), c_recv.at[3 + k])

    def c4():
        for k in range(4):
            arrived(first_row(k, 1 - c), c_recv.at[7 + k])

    tp_far = y * 2 + 1 - zh

    def spread_states(first, t):
        for i, y_ in enumerate((yr, yl, yo)):
            send(st.at[t], st.at[t], st_send.at[first + i], st_recv.at[first + i], device(y_=y_))

    e1(0, 0)
    locals_[3].wait()
    send(st.at[tp], st.at[tp], st_send.at[0], st_recv.at[0], device(zh_=1 - zh))
    z_start(0)
    spread_states(1, tp)
    locals_[7].wait()
    c1()
    locals_[4].wait()
    e1(1, 0)


    def one_length(r, carry):
        lens[pl.ds(r, 1), :] = jnp.full((1, 128), lengths[r], jnp.int32)
        return carry

    lax.fori_loop(0, 64, one_length, 0)

    def one_inverse(tb, carry):
        def look(b, found):
            return jnp.maximum(found, jnp.where(plan[b] == tb, b, 0))

        inverse[tb] = lax.fori_loop(0, 32, look, jnp.int32(0), unroll=32)
        return carry

    def some_inverse(n):
        lax.fori_loop(8 * n, 8 * n + 8, one_inverse, 0)

    e2(0, 0)
    c2()
    e2(1, 0)
    z_in(0, 1)
    z_in(0, 2)
    z_out(0, 1)
    e1(0, 1)
    arrived(st.at[tp_far], st_recv.at[0])
    spread_states(4, tp_far)
    e3(0, 0)
    e3(1, 0)
    z_in(0, 3)
    z_out(0, 2)
    e1(0, 2)
    e2(0, 1)
    e3(0, 1)
    z_out(0, 3)
    z_start(1)
    e1(0, 3)
    z_in(1, 1)
    z_in(1, 2)
    e2(0, 2)
    z_in(1, 3)
    c3()
    z_out(1, 1)
    e1(1, 1)
    e3(0, 2)
    z_out(1, 2)
    e1(1, 2)

    for first, zh_ in ((1, zh), (4, 1 - zh)):
        for i, y_ in enumerate((yl, yr, yo)):
            arrived(st.at[y_ * 2 + zh_], st_recv.at[first + i])

    def squares(t, total):
        wide = st[t].astype(F32)
        return total + jnp.sum(wide * wide, axis=-1, keepdims=True)

    total = lax.fori_loop(0, 8, squares, jnp.zeros((128, 1), F32))
    gain = lax.rsqrt(total / 8192.0 + 1e-05)

    def normalise(t, carry):
        for j in range(4):
            wide = st[t, :, 256 * j : 256 * (j + 1)].astype(F32)
            xn[t * 4 + j] = (wide * gain).astype(BF16)
        return carry

    lax.fori_loop(0, 8, normalise, 0)
    for k in range(4):
        for i in range(8):
            xp[k, :, 256 * i : 256 * (i + 1)] = xn[plan[zk[k] * 8 + i]]

    def project(k):
        e4(0, k)
        for n in range(3):
            cols = slice(256 * n, 256 * (n + 1))
            right = wa[k][:, :, cols].reshape(2048, 256)
            sums = jnp.dot(xp[k], right, preferred_element_type=F32)
            acc[:, cols] = sums if k == 0 else acc[:, cols] + sums

    project(0)
    project(1)
    project(2)
    c_in(1)
    c_in(2)
    e2(0, 3)
    z_out(1, 3)
    e1(1, 3)
    c_out(1)
    c_sibling(1)
    e3(0, 3)
    project(3)

    for s in range(2):
        rows = slice(64 * s, 64 * (s + 1))
        for g in range(4):
            piece = acc[rows, 128 * g : 128 * (g + 1)]
            q8[:, 4 * s + g, :] = piece.astype(BF16).astype(F32)
        for i in range(2):
            piece = acc[rows, 512 + 128 * i : 640 + 128 * i].astype(BF16)
            new_kv[s, i] = piece
            kvn[s, i] = piece.astype(F32)
    locals_[5].wait()
    locals_[6].wait()
    scale = 1.0 / 128**0.5

    def attend(n):
        rows = pl.ds(16 * n, 16)
        q = q8[rows]
        score = lax.dot_general(
            q.astype(BF16), keys[rows], (((2,), (2,)), ((0,), (0,))), preferred_element_type=F32
        ) * scale
        slots = lax.broadcasted_iota(jnp.int32, (16, 8, 128), 2)
        score = jnp.where(slots < lens[rows][:, None, :], score, -1e30)
        own = [
            jnp.sum(q * kvn[t, 0, rows][:, None, :], axis=-1, keepdims=True) * scale
            for t in range(2)
        ]
        second = lax.broadcasted_iota(jnp.int32, (16, 8, 1), 1) >= 4
        own[1] = jnp.where(second, own[1], -1e30)
        top = jnp.maximum(jnp.max(score, axis=-1, keepdims=True), jnp.maximum(own[0], own[1]))
        cached = jnp.exp(score - top)
        fresh = [jnp.exp(o - top) for o in own]
        total = jnp.sum(cached, axis=-1, keepdims=True) + fresh[0] + fresh[1]
        weight = (cached / total).astype(BF16)
        result = lax.dot_general(
            weight, values[rows], (((2,), (1,)), ((0,), (0,))), preferred_element_type=F32
        )
        for t in range(2):
            w = (fresh[t] / total).astype(BF16).astype(F32)
            result = result + w * kvn[t, 1, rows][:, None, :]
        h8[rows] = result

    e2(1, 1)
    attend(0)
    attend(1)
    c_in(3)
    e2(1, 2)
    attend(2)
    e3(1, 1)
    c_out(2)
    c_sibling(2)
    attend(3)

    for s in range(2):
        for g in range(4):
            heads[64 * s : 64 * (s + 1), 128 * g : 128 * (g + 1)] = h8[:, 4 * s + g, :].astype(BF16)
    some_inverse(0)
    e3(1, 2)
    some_inverse(1)
    e2(1, 3)
    some_inverse(2)
    some_inverse(3)
    c_out(3)
    c_sibling(3)
    e3(1, 3)

    for k in range(4):
        e4(1, k)
    c4()

    def product(j, t):
        b = inverse[t * 4 + j]
        low = jnp.dot(heads[:, :FIRST], wc[lax.rem(b, 2) * 16 + b // 2], preferred_element_type=F32)
        high = jnp.dot(heads[:, FIRST:], wb[b], preferred_element_type=F32)
        part[j, t] = (low + high).astype(BF16)

    def r_send_to(j, i, src, dst, to):
        send(src, dst, r_send.at[j, i], r_recv.at[j, i], to)

    to_left, to_right = device(y_=yl), device(y_=yr)

    def r1(j):
        product(j, yo * 2)
        r_send_to(j, 0, part.at[j, yo * 2], transit.at[j, 0], to_right)
        product(j, yo * 2 + 1)
        r_send_to(j, 1, part.at[j, yo * 2 + 1], transit.at[j, 1], to_left)
        product(j, yr * 2 + 1)
        r_send_to(j, 2, part.at[j, yr * 2 + 1], from_left.at[j, 1], to_right)
        product(j, yl * 2)
        r_send_to(j, 3, part.at[j, yl * 2], from_right.at[j, 0], to_left)
        product(j, yr * 2)
        product(j, yl * 2 + 1)
        product(j, y * 2)
        product(j, y * 2 + 1)

    def add(j, t, i):
        part[j, t] = (part[j, t].astype(F32) + transit[j, i].astype(F32)).astype(BF16)

    def r2(j):
        arrived(transit.at[j, 0], r_recv.at[j, 0])
        add(j, yr * 2, 0)
        r_send_to(j, 4, part.at[j, yr * 2], from_left.at[j, 0], to_right)
        arrived(transit.at[j, 1], r_recv.at[j, 1])
        add(j, yl * 2 + 1, 1)
        r_send_to(j, 5, part.at[j, yl * 2 + 1], from_right.at[j, 1], to_left)

    def summed(j, h):
        return (
            part[j, y * 2 + h].astype(F32) + from_left[j, h].astype(F32) + from_right[j, h].astype(F32)
        )

    def r3(j):
        arrived(from_left.at[j, 1], r_recv.at[j, 2])
        arrived(from_right.at[j, 0], r_recv.at[j, 3])
        arrived(from_left.at[j, 0], r_recv.at[j, 4])
        arrived(from_right.at[j, 1], r_recv.at[j, 5])
        far_out[j] = summed(j, 1 - zh).astype(BF16)
        r_send_to(j, 6, far_out.at[j], far_in.at[j], device(zh_=1 - zh))
        mine_sum[j] = summed(j, zh)

    r1(0)
    r1(1)
    r2(0)
    r1(2)
    r2(1)
    r3(0)
    r1(3)
    r2(2)
    r3(1)
    r2(3)
    r3(2)
    r3(3)
    for copy in sent[:-4]:
        copy.wait_send()

    @pl.when(inner)
    def _():
        for k in range(4):
            for t in range(2):
                z_copy(t, k).wait_send()
            c_copy(k).wait_send()

    for j in range(4):
        arrived(far_in.at[j], r_recv.at[j, 6])
        out[:, 256 * j : 256 * (j + 1)] = (mine_sum[j] + far_in[j].astype(F32)).astype(BF16)

    for copy in sent[-4:]:
        copy.wait_send()


def finish(sums, fresh, out, new_kv):
    out[...] = sums[...]
    new_kv[...] = fresh[...]


def on_device(states, cache, lengths, plan, wq_new, wkv_new, wo_new):
    vmem = pltpu.VMEM
    dma = pltpu.SemaphoreType.DMA
    hbm = pl.BlockSpec(memory_space=pltpu.HBM)
    smem = pl.BlockSpec(memory_space=pltpu.SMEM)
    attended, new_kv = pl.pallas_call(
        kernel,
        out_shape=(
            jax.ShapeDtypeStruct((128, 1024), BF16),
            jax.ShapeDtypeStruct((2, 2, 64, 128), BF16),
        ),
        in_specs=[smem, smem, hbm, hbm, hbm, hbm, hbm],
        out_specs=[pl.BlockSpec(memory_space=pltpu.VMEM)] * 2,
        scratch_shapes=[
            vmem((256, 512), BF16),
            vmem((2, 256, 128), BF16),
            *[vmem((8, 256, 768), BF16)] * 4,
            vmem((32, REST, 256), BF16),
            vmem((32, FIRST, 256), BF16),
            vmem((8, 128, 1024), BF16),
            vmem((32, 128, 256), BF16),
            vmem((4, 128, 2048), BF16),
            vmem((128, 768), F32),
            vmem((64, 128, 128), BF16),
            vmem((64, 128, 128), BF16),
            vmem((64, 128), jnp.int32),
            vmem((64, 8, 128), F32),
            vmem((64, 8, 128), F32),
            vmem((128, 512), BF16),
            vmem((2, 2, 64, 128), F32),
            pltpu.SMEM((32,), jnp.int32),
            vmem((4, 8, 128, 256), BF16),
            vmem((4, 2, 128, 256), BF16),
            vmem((4, 2, 128, 256), BF16),
            vmem((4, 2, 128, 256), BF16),
            vmem((4, 128, 256), BF16),
            vmem((4, 128, 256), BF16),
            vmem((4, 128, 256), F32),
            dma((8,)),
            dma((7,)), dma((7,)),
            dma((2, 35)), dma((2, 35)), dma((2, 4)),
            dma((11,)), dma((11,)), dma((4,)),
            dma((4, 7)), dma((4, 7)),
        ],
        compiler_params=pltpu.CompilerParams(
            collective_id=0, has_side_effects=True, vmem_limit_bytes=60 * 2**20
        ),
        name="layer",
    )(
        plan, lengths, states.reshape(128, 1024), cache.reshape(2, 64, 128, 128),
        wq_new, wkv_new, wo_new,
    )
    whole = pl.BlockSpec(memory_space=pltpu.VMEM)
    attended, new_kv = pl.pallas_call(
        finish,
        out_shape=(
            jax.ShapeDtypeStruct((128, 1024), BF16),
            jax.ShapeDtypeStruct((2, 2, 64, 128), BF16),
        ),
        in_specs=[whole, whole],
        out_specs=[whole, whole],
        name="finish",
    )(attended, new_kv)
    return attended.reshape(2, 64, 1024), new_kv.reshape(2, 2, 64, 1, 128)


def solution(mesh):
    return jax.shard_map(
        on_device,
        mesh=mesh,
        in_specs=(
            P(None, "grp", "tp"),
            P(None, "grp", "tp", None, None),
            P("grp"),
            P(),
            P("grp", "tp"),
            P(None, "grp", "tp"),
            P("tp", "grp"),
        ),
        out_specs=(P(None, "grp", "tp"), P(None, None, "grp", "tp", None)),
        check_vma=False,
    )
```

```python
import functools

import jax
import jax.numpy as jnp
from jax import lax
from jax.experimental import pallas as pl
from jax.experimental.pallas import tpu as pltpu
from jax.sharding import PartitionSpec as P

MESH = pl.DeviceIdType.MESH
FIRST = 192
REST = 512 - FIRST
F32 = jnp.float32
BF16 = jnp.bfloat16


def kernel(
    plan, lengths, states, cache, wq, wkv, wo,
    out, new_kv,
    own_q, own_kv,
    wa0, wa1, wa2, wa3, wb, wc, st, xn, xp, acc, keys, values, lens, q8, h8, heads, kvn, inverse,
    part, from_left, from_right, transit, far_out, far_in,
    local_sem, st_send, st_recv, w_send, w_recv, z_send, c_send, c_recv, cz_send, r_send, r_recv,
):
    grp = lax.axis_index("grp")
    tp = lax.axis_index("tp")
    z, x, c = grp // 8, lax.rem(grp // 2, 4), lax.rem(grp, 2)
    y, zh = tp // 2, lax.rem(tp, 2)

    def mod4(v):
        return lax.rem(v + 4, 4)

    def block_of(z_, x_, c_):
        return (z_ * 4 + x_) * 2 + c_

    def device(x_=x, y_=y, z_=z, zh_=zh, c_=c):
        return (block_of(z_, x_, c_), y_ * 2 + zh_)

    xl, xr, xo = mod4(x - 1), mod4(x + 1), mod4(x + 2)
    yl, yr, yo = mod4(y - 1), mod4(y + 1), mod4(y + 2)
    z_pair, z_mirror = z + 1 - 2 * lax.rem(z, 2), 3 - z
    upper = z // 2
    inner = lax.rem(z + 1, 4) // 2 == 1
    zk = [z, z_pair, 2 - upper, 3 - 3 * upper]

    locals_ = [
        pltpu.make_async_copy(wq, own_q, local_sem.at[0]),
        pltpu.make_async_copy(wkv.at[0], own_kv.at[0], local_sem.at[1]),
        pltpu.make_async_copy(wkv.at[1], own_kv.at[1], local_sem.at[2]),
        pltpu.make_async_copy(states, st.at[tp], local_sem.at[3]),
        pltpu.make_async_copy(wo.at[pl.ds(FIRST, REST)], wb.at[grp], local_sem.at[4]),
        pltpu.make_async_copy(cache.at[0], keys, local_sem.at[5]),
        pltpu.make_async_copy(cache.at[1], values, local_sem.at[6]),
        pltpu.make_async_copy(wo.at[pl.ds(0, FIRST)], wc.at[c * 16 + z * 4 + x], local_sem.at[7]),
    ]
    for copy in locals_:
        copy.start()

    partners = [
        device(x_=xl), device(x_=xr), device(c_=1 - c),
        device(y_=yl), device(y_=yr), device(y_=yo), device(zh_=1 - zh),
        device(z_=z_pair), device(z_=z_mirror),
    ]
    barrier = pltpu.get_barrier_semaphore()
    for partner in partners:
        pl.semaphore_signal(barrier, inc=1, device_id=partner, device_id_type=MESH)
    for i in (0, 1, 2):
        locals_[i].wait()
    mine = x * 2 + c
    wa0[mine, :, 0:512] = own_q[...]
    wa0[mine, :, 512:640] = own_kv[0]
    wa0[mine, :, 640:768] = own_kv[1]
    pl.semaphore_wait(barrier, len(partners))

    sent = []

    def send(src, dst, send_sem, recv_sem, to):
        copy = pltpu.make_async_remote_copy(
            src_ref=src, dst_ref=dst, send_sem=send_sem, recv_sem=recv_sem,
            device_id=to, device_id_type=MESH,
        )
        copy.start()
        sent.append(copy)

    def arrived(dst, recv_sem):
        pltpu.make_async_remote_copy(
            src_ref=dst, dst_ref=dst, send_sem=recv_sem, recv_sem=recv_sem,
            device_id=device(c_=1 - c), device_id_type=MESH,
        ).wait_recv()

    wa = (wa0, wa1, wa2, wa3)

    def held(t, k, x_, c_, there=None):
        if t == 0:
            return wa[k if there is None else there].at[x_ * 2 + c_]
        return wb.at[block_of(zk[k], x_, c_)]

    halves = (128, REST // 2)

    def z_start(t):
        send(held(t, 0, x, c), held(t, 0, x, c, 1), w_send.at[t, 0], w_recv.at[t, 0], device(z_=z_pair))
        pl.when(inner)(lambda: z_copy(t, 0).start())

    def z_copy(t, k):
        there = k + 2 if k < 2 else k
        return pltpu.make_async_remote_copy(
            src_ref=held(t, k, x, c), dst_ref=held(t, k, x, c, there),
            send_sem=z_send.at[t, k], recv_sem=w_recv.at[t, there - 1],
            device_id=device(z_=z_mirror) if k < 2 else device(z_=z_pair), device_id_type=MESH,
        )

    def z_in(t, k):
        @pl.when(inner)
        def _():
            arrived(held(t, k, x, c), w_recv.at[t, k - 1])
            z_copy(t, k).start()

    def z_out(t, k):
        @pl.when(jnp.logical_not(inner))
        def _():
            arrived(held(t, k, x, c), w_recv.at[t, k - 1])

    def base(k):
        return 3 + 8 * k

    def sibling(t, k, i, ref):
        s = base(k) + 4 + i
        send(ref, ref, w_send.at[t, s], w_recv.at[t, s], device(c_=1 - c))

    def e1(t, k):
        ref = held(t, k, x, c)
        s = base(k)
        send(ref, ref, w_send.at[t, s], w_recv.at[t, s], device(x_=xr))
        send(ref, ref, w_send.at[t, s + 1], w_recv.at[t, s + 1], device(x_=xl))
        sibling(t, k, 0, ref)

    def e2(t, k):
        s = base(k)
        half = halves[t]
        for i, x_, to, rows in ((0, xl, xr, pl.ds(0, half)), (1, xr, xl, pl.ds(half, half))):
            ref = held(t, k, x_, c)
            arrived(ref, w_recv.at[t, s + i])
            part_ref = ref.at[rows]
            send(part_ref, part_ref, w_send.at[t, s + 2 + i], w_recv.at[t, s + 2 + i], device(x_=to))
            sibling(t, k, 1 + i, ref)

    def e3(t, k):
        s = base(k)
        half = halves[t]
        ref = held(t, k, xo, c)
        arrived(ref.at[pl.ds(0, half)], w_recv.at[t, s + 2])
        arrived(ref.at[pl.ds(half, half)], w_recv.at[t, s + 3])
        sibling(t, k, 3, ref)

    def e4(t, k):
        for i, x_ in enumerate((x, xl, xr, xo)):
            arrived(held(t, k, x_, 1 - c), w_recv.at[t, base(k) + 4 + i])

    def first_of(z_, x_, c_):
        return c_ * 16 + z_ * 4 + x_

    def first_row(k, c_):
        return wc.at[pl.ds(first_of(zk[k], 0, c_), 4)]

    def c1():
        ref = wc.at[first_of(z, x, c)]
        send(ref, ref, c_send.at[0], c_recv.at[0], device(x_=xr))
        send(ref, ref, c_send.at[1], c_recv.at[1], device(x_=xl))

    def c2():
        half = FIRST // 2
        for i, x_, to, rows in ((0, xl, xr, pl.ds(0, half)), (1, xr, xl, pl.ds(half, half))):
            n = first_of(z, x_, c)
            arrived(wc.at[n], c_recv.at[i])
            ref = wc.at[n, rows]
            send(ref, ref, c_send.at[2 + i], c_recv.at[2 + i], device(x_=to))

    def c_copy(k):
        ref = first_row(k, c)
        arrives = 5 + k if k < 2 else 3 + k
        return pltpu.make_async_remote_copy(
            src_ref=ref, dst_ref=ref, send_sem=cz_send.at[k], recv_sem=c_recv.at[arrives],
            device_id=device(z_=z_mirror) if k < 2 else device(z_=z_pair), device_id_type=MESH,
        )

    def c_sibling(k):
        ref = first_row(k, c)
        send(ref, ref, c_send.at[7 + k], c_recv.at[7 + k], device(c_=1 - c))

    def c3():
        half = FIRST // 2
        n = first_of(z, xo, c)
        arrived(wc.at[n, pl.ds(0, half)], c_recv.at[2])
        arrived(wc.at[n, pl.ds(half, half)], c_recv.at[3])
        ref = first_row(0, c)
        send(ref, ref, c_send.at[4], c_recv.at[4], device(z_=z_pair))
        pl.when(inner)(lambda: c_copy(0).start())
        c_sibling(0)

    def c_in(k):
        @pl.when(inner)
        def _():
            arrived(first_row(k, c), c_recv.at[3 + k])
            c_copy(k).start()

    def c_out(k):
        @pl.when(jnp.logical_not(inner))
        def _():
            arrived(first_row(k, c), c_recv.at[3 + k])

    def c4():
        for k in range(4):
            arrived(first_row(k, 1 - c), c_recv.at[7 + k])

    tp_far = y * 2 + 1 - zh

    def spread_states(first, t):
        for i, y_ in enumerate((yr, yl, yo)):
            send(st.at[t], st.at[t], st_send.at[first + i], st_recv.at[first + i], device(y_=y_))

    e1(0, 0)
    locals_[3].wait()
    send(st.at[tp], st.at[tp], st_send.at[0], st_recv.at[0], device(zh_=1 - zh))
    z_start(0)
    spread_states(1, tp)
    locals_[7].wait()
    c1()
    locals_[4].wait()
    e1(1, 0)


    def one_length(r, carry):
        lens[pl.ds(r, 1), :] = jnp.full((1, 128), lengths[r], jnp.int32)
        return carry

    lax.fori_loop(0, 64, one_length, 0)

    def one_inverse(tb, carry):
        def look(b, found):
            return jnp.maximum(found, jnp.where(plan[b] == tb, b, 0))

        inverse[tb] = lax.fori_loop(0, 32, look, jnp.int32(0), unroll=32)
        return carry

    def some_inverse(n):
        lax.fori_loop(8 * n, 8 * n + 8, one_inverse, 0)

    e2(0, 0)
    c2()
    e2(1, 0)
    z_in(0, 1)
    z_in(0, 2)
    z_out(0, 1)
    e1(0, 1)
    some_inverse(0)
    arrived(st.at[tp_far], st_recv.at[0])
    spread_states(4, tp_far)
    e3(0, 0)
    e3(1, 0)
    z_in(0, 3)
    z_out(0, 2)
    e1(0, 2)
    some_inverse(1)
    e2(0, 1)
    e3(0, 1)
    z_out(0, 3)
    z_start(1)
    e1(0, 3)
    some_inverse(2)
    z_in(1, 1)
    z_in(1, 2)
    e2(0, 2)
    z_in(1, 3)
    c3()
    z_out(1, 1)
    e1(1, 1)
    some_inverse(3)
    e3(0, 2)
    z_out(1, 2)
    e1(1, 2)

    for first, zh_ in ((1, zh), (4, 1 - zh)):
        for i, y_ in enumerate((yl, yr, yo)):
            arrived(st.at[y_ * 2 + zh_], st_recv.at[first + i])

    def squares(t, total):
        wide = st[t].astype(F32)
        return total + jnp.sum(wide * wide, axis=-1, keepdims=True)

    total = lax.fori_loop(0, 8, squares, jnp.zeros((128, 1), F32))
    gain = lax.rsqrt(total / 8192.0 + 1e-05)

    def normalise(t, carry):
        for j in range(4):
            wide = st[t, :, 256 * j : 256 * (j + 1)].astype(F32)
            xn[t * 4 + j] = (wide * gain).astype(BF16)
        return carry

    lax.fori_loop(0, 8, normalise, 0)
    for k in range(4):
        for i in range(8):
            xp[k, :, 256 * i : 256 * (i + 1)] = xn[plan[zk[k] * 8 + i]]

    def project(k):
        e4(0, k)
        for n in range(3):
            cols = slice(256 * n, 256 * (n + 1))
            right = wa[k][:, :, cols].reshape(2048, 256)
            sums = jnp.dot(xp[k], right, preferred_element_type=F32)
            acc[:, cols] = sums if k == 0 else acc[:, cols] + sums

    project(0)
    project(1)
    project(2)
    c_in(1)
    c_in(2)
    e2(0, 3)
    z_out(1, 3)
    e1(1, 3)
    c_out(1)
    c_sibling(1)
    e3(0, 3)
    project(3)

    for s in range(2):
        rows = slice(64 * s, 64 * (s + 1))
        for g in range(4):
            piece = acc[rows, 128 * g : 128 * (g + 1)]
            q8[:, 4 * s + g, :] = piece.astype(BF16).astype(F32)
        for i in range(2):
            piece = acc[rows, 512 + 128 * i : 640 + 128 * i].astype(BF16)
            new_kv[s, i] = piece
            kvn[s, i] = piece.astype(F32)
    locals_[5].wait()
    locals_[6].wait()
    scale = 1.0 / 128**0.5

    def attend(n):
        rows = pl.ds(16 * n, 16)
        q = q8[rows]
        score = lax.dot_general(
            q.astype(BF16), keys[rows], (((2,), (2,)), ((0,), (0,))), preferred_element_type=F32
        ) * scale
        slots = lax.broadcasted_iota(jnp.int32, (16, 8, 128), 2)
        score = jnp.where(slots < lens[rows][:, None, :], score, -1e30)
        own = [
            jnp.sum(q * kvn[t, 0, rows][:, None, :], axis=-1, keepdims=True) * scale
            for t in range(2)
        ]
        second = lax.broadcasted_iota(jnp.int32, (16, 8, 1), 1) >= 4
        own[1] = jnp.where(second, own[1], -1e30)
        top = jnp.maximum(jnp.max(score, axis=-1, keepdims=True), jnp.maximum(own[0], own[1]))
        cached = jnp.exp(score - top)
        fresh = [jnp.exp(o - top) for o in own]
        total = jnp.sum(cached, axis=-1, keepdims=True) + fresh[0] + fresh[1]
        weight = (cached / total).astype(BF16)
        result = lax.dot_general(
            weight, values[rows], (((2,), (1,)), ((0,), (0,))), preferred_element_type=F32
        )
        for t in range(2):
            w = (fresh[t] / total).astype(BF16).astype(F32)
            result = result + w * kvn[t, 1, rows][:, None, :]
        h8[rows] = result

    e2(1, 1)
    attend(0)
    attend(1)
    c_in(3)
    e2(1, 2)
    attend(2)
    e3(1, 1)
    c_out(2)
    c_sibling(2)
    attend(3)

    for s in range(2):
        for g in range(4):
            heads[64 * s : 64 * (s + 1), 128 * g : 128 * (g + 1)] = h8[:, 4 * s + g, :].astype(BF16)
    e3(1, 2)
    e2(1, 3)
    c_out(3)
    c_sibling(3)
    e3(1, 3)

    for k in range(4):
        e4(1, k)
    c4()

    def product(j, t):
        b = inverse[t * 4 + j]
        low = jnp.dot(heads[:, :FIRST], wc[lax.rem(b, 2) * 16 + b // 2], preferred_element_type=F32)
        high = jnp.dot(heads[:, FIRST:], wb[b], preferred_element_type=F32)
        part[j, t] = (low + high).astype(BF16)

    def r_send_to(j, i, src, dst, to):
        send(src, dst, r_send.at[j, i], r_recv.at[j, i], to)

    to_left, to_right = device(y_=yl), device(y_=yr)

    def r1(j):
        product(j, yo * 2)
        r_send_to(j, 0, part.at[j, yo * 2], transit.at[j, 0], to_right)
        product(j, yo * 2 + 1)
        r_send_to(j, 1, part.at[j, yo * 2 + 1], transit.at[j, 1], to_left)
        product(j, yr * 2 + 1)
        r_send_to(j, 2, part.at[j, yr * 2 + 1], from_left.at[j, 1], to_right)
        product(j, yl * 2)
        r_send_to(j, 3, part.at[j, yl * 2], from_right.at[j, 0], to_left)
        product(j, yr * 2)
        product(j, yl * 2 + 1)
        product(j, y * 2)
        product(j, y * 2 + 1)

    def add(j, t, i):
        part[j, t] = (part[j, t].astype(F32) + transit[j, i].astype(F32)).astype(BF16)

    def r2(j):
        arrived(transit.at[j, 0], r_recv.at[j, 0])
        add(j, yr * 2, 0)
        r_send_to(j, 4, part.at[j, yr * 2], from_left.at[j, 0], to_right)
        arrived(transit.at[j, 1], r_recv.at[j, 1])
        add(j, yl * 2 + 1, 1)
        r_send_to(j, 5, part.at[j, yl * 2 + 1], from_right.at[j, 1], to_left)

    def summed(j, h):
        return (
            part[j, y * 2 + h].astype(F32) + from_left[j, h].astype(F32) + from_right[j, h].astype(F32)
        )

    def r3(j):
        arrived(from_left.at[j, 1], r_recv.at[j, 2])
        arrived(from_right.at[j, 0], r_recv.at[j, 3])
        arrived(from_left.at[j, 0], r_recv.at[j, 4])
        arrived(from_right.at[j, 1], r_recv.at[j, 5])
        far_out[j] = summed(j, 1 - zh).astype(BF16)
        r_send_to(j, 6, far_out.at[j], far_in.at[j], device(zh_=1 - zh))

    r1(0)
    r1(1)
    r2(0)
    r1(2)
    r2(1)
    r3(0)
    r1(3)
    r2(2)
    r3(1)
    r2(3)
    r3(2)
    r3(3)
    for copy in sent[:-4]:
        copy.wait_send()

    @pl.when(inner)
    def _():
        for k in range(4):
            for t in range(2):
                z_copy(t, k).wait_send()
            c_copy(k).wait_send()

    for j in range(4):
        arrived(far_in.at[j], r_recv.at[j, 6])
        out[:, 256 * j : 256 * (j + 1)] = (summed(j, zh) + far_in[j].astype(F32)).astype(BF16)

    for copy in sent[-4:]:
        copy.wait_send()


def finish(sums, fresh, out, new_kv):
    out[...] = sums[...]
    new_kv[...] = fresh[...]


def on_device(states, cache, lengths, plan, wq_new, wkv_new, wo_new):
    vmem = pltpu.VMEM
    dma = pltpu.SemaphoreType.DMA
    hbm = pl.BlockSpec(memory_space=pltpu.HBM)
    smem = pl.BlockSpec(memory_space=pltpu.SMEM)
    attended, new_kv = pl.pallas_call(
        kernel,
        out_shape=(
            jax.ShapeDtypeStruct((128, 1024), BF16),
            jax.ShapeDtypeStruct((2, 2, 64, 128), BF16),
        ),
        in_specs=[smem, smem, hbm, hbm, hbm, hbm, hbm],
        out_specs=[pl.BlockSpec(memory_space=pltpu.VMEM)] * 2,
        scratch_shapes=[
            vmem((256, 512), BF16),
            vmem((2, 256, 128), BF16),
            *[vmem((8, 256, 768), BF16)] * 4,
            vmem((32, REST, 256), BF16),
            vmem((32, FIRST, 256), BF16),
            vmem((8, 128, 1024), BF16),
            vmem((32, 128, 256), BF16),
            vmem((4, 128, 2048), BF16),
            vmem((128, 768), F32),
            vmem((64, 128, 128), BF16),
            vmem((64, 128, 128), BF16),
            vmem((64, 128), jnp.int32),
            vmem((64, 8, 128), F32),
            vmem((64, 8, 128), F32),
            vmem((128, 512), BF16),
            vmem((2, 2, 64, 128), F32),
            pltpu.SMEM((32,), jnp.int32),
            vmem((4, 8, 128, 256), BF16),
            vmem((4, 2, 128, 256), BF16),
            vmem((4, 2, 128, 256), BF16),
            vmem((4, 2, 128, 256), BF16),
            vmem((4, 128, 256), BF16),
            vmem((4, 128, 256), BF16),
            dma((8,)),
            dma((7,)), dma((7,)),
            dma((2, 35)), dma((2, 35)), dma((2, 4)),
            dma((11,)), dma((11,)), dma((4,)),
            dma((4, 7)), dma((4, 7)),
        ],
        compiler_params=pltpu.CompilerParams(
            collective_id=0, has_side_effects=True, vmem_limit_bytes=60 * 2**20
        ),
        name="layer",
    )(
        plan, lengths, states.reshape(128, 1024), cache.reshape(2, 64, 128, 128),
        wq_new, wkv_new, wo_new,
    )
    whole = pl.BlockSpec(memory_space=pltpu.VMEM)
    attended, new_kv = pl.pallas_call(
        finish,
        out_shape=(
            jax.ShapeDtypeStruct((128, 1024), BF16),
            jax.ShapeDtypeStruct((2, 2, 64, 128), BF16),
        ),
        in_specs=[whole, whole],
        out_specs=[whole, whole],
        name="finish",
    )(attended, new_kv)
    return attended.reshape(2, 64, 1024), new_kv.reshape(2, 2, 64, 1, 128)


def solution(mesh):
    return jax.shard_map(
        on_device,
        mesh=mesh,
        in_specs=(
            P(None, "grp", "tp"),
            P(None, "grp", "tp", None, None),
            P("grp"),
            P(),
            P("grp", "tp"),
            P(None, "grp", "tp"),
            P("tp", "grp"),
        ),
        out_specs=(P(None, "grp", "tp"), P(None, None, "grp", "tp", None)),
        check_vma=False,
    )
```
